128 devices in a mesh: group: 8 (over x, core), member: 16 (over y, z).
Axes of the slice: x: 4, y: 4, z: 4, core: 2. Of those that a mesh axis runs over, the one named last changes fastest.
Arguments:
- root_front: float32 [8192, 8192], P('member', 'group'), may hold values from -6 to 6
- child_panels: bfloat16 [8, 4096, 4096], P('group', 'member'), may hold values from -1.75 to 1.75
- pivot_sizes: float32 [8, 4096], P('group'), may hold values from 0.02 to 4
- pivot_signs: int32 [8, 4096], P('group'), may hold values from 0 to 1
- child_blocks: int32 [8, 32], replicated, may hold values from 0 to 63, as said below
Outputs:
- updated_front: float32 [8192, 8192], P('member', 'group')
The draws below stay inside these ranges and needn't reach their ends.
Inputs may be any that keep to these rules, and one draw needn't show every extreme that they name: Each row child_blocks[g] holds 32 distinct root blocks in increasing order, exactly 2 of them in each run of root blocks k * 4 to (k + 1) * 4 - 1.
All inputs are finite; a program needn't handle non-finite values.
Results may differ from the reference program's by a relative error of at most 0.0044.
Values may be sent and summed in bfloat16 or wider, within the bound.
A program may use at most 128 MiB of HBM per device.

```python
import math
import jax
import jax.numpy as jnp
from jax import lax

B = 128
S = 8192
W = 4096
R = 4096
NRB = 32
NPB = 4
KEEP = 2
N_GROUP = 8
N_MEMBER = 16


def draw_child_blocks(key, part):
    key = jax.random.fold_in(key, 7)
    scores = jax.random.randint(key, (N_GROUP, N_MEMBER, NPB), 0, 1 << 20)
    scores = scores * NPB + jnp.arange(NPB, dtype=jnp.int32)[None, None, :]
    scores = scores.at[:, 0, 0].set(-1)
    scores = scores.at[:, N_MEMBER - 1, NPB - 1].set(-1)
    order = jnp.argsort(scores, axis=-1)
    chosen = jnp.sort(order[:, :, :KEEP], axis=-1)
    starts = jnp.arange(N_MEMBER, dtype=jnp.int32)[None, :, None] * NPB
    return (chosen + starts).reshape(N_GROUP, NRB).astype(jnp.int32)


def with_ends(drawn, rng, low, largest):
    longest = drawn.shape.index(max(drawn.shape))
    spots = []
    for shift in (0, 1):
        where = [jax.random.randint(jax.random.fold_in(rng, axis), (), 0, length) for axis, length in enumerate(drawn.shape)]
        where[longest] = (where[longest] + shift) % drawn.shape[longest]
        spots.append(tuple(where))
    return drawn.at[spots[0]].set(low).at[spots[1]].set(largest)


def steps_of(rng, extent, shards, smallest, top_value):
    def one(axis_at, blocks):
        heights = jax.random.uniform(jax.random.fold_in(jax.random.fold_in(rng, 6), axis_at), (blocks,), jnp.float32, smallest / len(shards), top_value / len(shards))
        return jnp.repeat(jnp.exp(heights), extent[axis_at] // blocks).reshape((-1,) + (1,) * (len(extent) - axis_at - 1))

    loudness = one(*shards[0])
    for cut in shards[1:]:
        loudness = loudness * one(*cut)
    return loudness


def bell_draw(rng, shape, deviation, reach, shards=(), kind=jnp.bfloat16):
    gain = steps_of(rng, shape, shards, -0.22, 0.18) if shards else 1.0
    array = jax.random.normal(rng, shape, jnp.float32) * deviation * gain
    return jnp.minimum(jnp.maximum(array, -reach), reach).astype(kind)


def setup_inputs(seed: int = 0) -> dict:
    seeds = jax.random.split(jax.random.key(seed), 6)
    return {
        "root_front": bell_draw(seeds[0], (S, S), 1.0, 6.0, ((0, 16), (1, 8)), jnp.float32),
        "child_panels": bell_draw(seeds[1], (N_GROUP, R, W), 0.116, 1.75, ((0, 8), (1, 16))),
        "pivot_sizes": jnp.clip(jnp.exp(math.log(4.0) - 5.2983174 * jax.random.uniform(seeds[2], (N_GROUP, W), jnp.float32) ** steps_of(seeds[2], (N_GROUP, W), ((0, 8),), -0.2, 0.2)), 0.02, 4.0),
        "pivot_signs": with_ends(jax.random.randint(seeds[3], (N_GROUP, W), 0, 2), jax.random.fold_in(seeds[3], 1), 0, 1).astype(jnp.int32),
        "child_blocks": draw_child_blocks(jax.random.fold_in(seeds[5], 71), 0),
    }


pivot_floor = 0.1

def reference(root_front, child_panels, pivot_sizes, pivot_signs, child_blocks):
    clipped = jnp.maximum(pivot_sizes, pivot_floor)
    sign_vals = (2 * pivot_signs - 1).astype(jnp.float32)
    scaled = (child_panels.astype(jnp.float32) * jnp.sqrt(clipped)[:, None, :]).astype(jnp.bfloat16)
    offsets = jnp.arange(B, dtype=jnp.int32)
    contract = (((1,), (1,)), ((), ()))

    def add_group(root_sum, inputs):
        panel_in, sign_in, block_list = inputs
        signed = (panel_in.astype(jnp.float32) * sign_in[None, :]).astype(jnp.bfloat16)
        update = lax.dot_general(signed, panel_in, contract, preferred_element_type=jnp.float32)
        row_index = (block_list[:, None] * B + offsets[None, :]).reshape(-1).astype(jnp.int32)
        root_sum = root_sum.at[row_index[:, None], row_index[None, :]].add(-update)
        return (root_sum, None)
    result, unused = lax.scan(add_group, root_front, (scaled, sign_vals, child_blocks))
    return result
```

```python
import jax
import jax.numpy as jnp
from jax import lax
from jax.experimental import pallas as pl
from jax.experimental.pallas import tpu as pltpu
from jax.sharding import PartitionSpec as P

B = 128
ROWS = 256
K = 4096
NC = 8
KC = K // NC
SIDE = 4
pivot_floor = 0.1

TRI = ((0, 0), (0, 1), (1, 0), (1, 1), (0, 2), (2, 0))
PAIRS = (
    (0, 0, False),
    (0, 1, True),
    (0, 2, True),
    (2, 1, True),
    (0, 3, True),
    (0, 4, False),
    (2, 4, True),
    (0, 5, False),
    (5, 1, True),
    (5, 4, False),
)


def dot_nt(left, right):
    return lax.dot_general(left, right, (((1,), (1,)), ((), ())), preferred_element_type=jnp.float32)


def meet_kernel(panel, sizes, signs, arrived, pan, acc, stage, load_sem, hop_send, hop_recv, tile_send, tile_recv):
    group = lax.axis_index("group")
    member = lax.axis_index("member")
    row, col = member // SIDE, member % SIDE
    turn = 1 - 2 * (group % 2)

    def at(offset):
        y = (row + turn * offset[0] + SIDE) % SIDE
        z = (col + turn * offset[1] + SIDE) % SIDE
        return y * SIDE + z

    to_z, to_y = at((0, -1)), at((-1, 0))

    def cols(k):
        return pl.ds(pl.multiple_of(k * KC, KC), KC)

    def load(k):
        return pltpu.make_async_copy(panel.at[0, :, cols(k)], pan.at[0, :, cols(k)], load_sem.at[k])

    def hop(src, dst, k, target):
        return pltpu.make_async_remote_copy(
            src_ref=pan.at[src, :, cols(k)],
            dst_ref=pan.at[dst, :, cols(k)],
            send_sem=hop_send.at[dst - 1, k],
            recv_sem=hop_recv.at[dst - 1, k],
            device_id={"group": group, "member": target},
            device_id_type=pl.DeviceIdType.MESH,
        )

    def hop_corner(k):
        return hop(2, 3, k, to_z) if k % 2 == 0 else hop(1, 3, k, to_y)

    def each(body):
        lax.fori_loop(0, NC, lambda k, c: (body(k), c)[1], 0)

    for k in range(NC):
        load(k).start()

    root = jnp.sqrt(jnp.maximum(sizes[...], pivot_floor))
    sign = (2 * signs[...] - 1).astype(jnp.float32).astype(jnp.bfloat16)
    sizes_root, sign_row = root, sign

    for k in range(NC):
        load(k).wait()
        s = slice(k * KC, (k + 1) * KC)
        pan[0, :, s] = (pan[0, :, s].astype(jnp.float32) * sizes_root[:, s]).astype(jnp.bfloat16)
        hop(0, 1, k, to_z).start()
        hop(0, 2, k, to_y).start()

    def signed(slot, k):
        s = (2 * signs[:, cols(k)] - 1).astype(jnp.float32).astype(jnp.bfloat16)
        return pan[slot, :, cols(k)] * s

    def accumulate(n, left, right, k):
        prod = dot_nt(left, pan[right, :, cols(k)])

        @pl.when(k == 0)
        def _():
            acc[n] = prod

        @pl.when(k > 0)
        def _():
            acc[n] += prod

    def send_copies():
        out = []
        slot = 0
        for n, (a, b, both) in enumerate(PAIRS):
            for r, c in ((a, b), (b, a)) if both else ((a, b),):
                row_at, col_at = at(TRI[r]), at(TRI[c])
                out.append((n, slot, r, c, (r, c) != (a, b), row_at, col_at))
                slot += 1
        return out

    copies = send_copies()

    def tile(slot, row_at, col_at):
        return pltpu.make_async_remote_copy(
            src_ref=stage.at[slot],
            dst_ref=arrived.at[group, col_at % 2],
            send_sem=tile_send.at[slot],
            recv_sem=tile_recv.at[group, col_at % 2],
            device_id={"group": col_at // 2, "member": row_at},
            device_id_type=pl.DeviceIdType.MESH,
        )

    def tile_here(slot, col_at):
        return pltpu.make_async_copy(stage.at[slot], arrived.at[group, col_at % 2], tile_recv.at[group, col_at % 2])

    def ship(n):
        for m, slot, r, c, flipped, row_at, col_at in copies:
            if m != n:
                continue
            value = acc[n]
            stage[slot] = (value.T if flipped else value).astype(jnp.bfloat16)
            if r == 0:
                here = col_at // 2 == group

                @pl.when(here)
                def _():
                    tile_here(slot, col_at).start()

                @pl.when(jnp.logical_not(here))
                def _():
                    tile(slot, row_at, col_at).start()
            else:
                tile(slot, row_at, col_at).start()

    def first(k):
        own = signed(0, k)
        accumulate(0, own, 0, k)
        hop(0, 1, k, to_z).wait_recv()
        hop(0, 2, k, to_y).wait_recv()
        accumulate(1, own, 1, k)
        accumulate(2, own, 2, k)
        accumulate(3, signed(2, k), 1, k)

    each(first)
    for k in range(NC):
        hop_corner(k).start()
    for k in range(NC):
        hop(1, 4, k, to_z).start()
        hop(2, 5, k, to_y).start()
    for n in range(4):
        ship(n)

    def corner(k):
        hop(2, 3, k, to_z).wait_recv()
        accumulate(4, signed(0, k), 3, k)

    each(corner)
    ship(4)

    def far(k):
        hop(1, 4, k, to_z).wait_recv()
        hop(2, 5, k, to_y).wait_recv()
        own = signed(0, k)
        accumulate(5, own, 4, k)
        accumulate(6, signed(2, k), 4, k)
        accumulate(7, own, 5, k)
        last = signed(5, k)
        accumulate(8, last, 1, k)
        accumulate(9, last, 4, k)

    each(far)
    for n in range(5, 10):
        ship(n)

    def drain(k):
        hop(0, 1, k, to_z).wait_send()
        hop(0, 2, k, to_y).wait_send()
        hop(2, 3, k, to_z).wait_send()
        hop(1, 4, k, to_z).wait_send()
        hop(2, 5, k, to_y).wait_send()

    each(drain)
    for _, slot, r, c, _, row_at, col_at in copies:
        if r == 0:

            @pl.when(col_at // 2 != group)
            def _():
                tile(slot, row_at, col_at).wait_send()
        else:
            tile(slot, row_at, col_at).wait_send()
    for g in range(8):
        for j in range(2):
            pltpu.make_async_copy(stage.at[0], arrived.at[g, j], tile_recv.at[g, j]).wait()


def meet(panel, sizes, signs):
    return pl.pallas_call(
        meet_kernel,
        out_shape=jax.ShapeDtypeStruct((8, 2, ROWS, ROWS), jnp.bfloat16),
        in_specs=[
            pl.BlockSpec(memory_space=pl.ANY),
            pl.BlockSpec(memory_space=pltpu.VMEM),
            pl.BlockSpec(memory_space=pltpu.VMEM),
        ],
        out_specs=pl.BlockSpec(memory_space=pl.ANY),
        scratch_shapes=[
            pltpu.VMEM((6, ROWS, K), jnp.bfloat16),
            pltpu.VMEM((10, ROWS, ROWS), jnp.float32),
            pltpu.VMEM((16, ROWS, ROWS), jnp.bfloat16),
            pltpu.SemaphoreType.DMA((NC,)),
            pltpu.SemaphoreType.DMA((5, NC)),
            pltpu.SemaphoreType.DMA((5, NC)),
            pltpu.SemaphoreType.DMA((16,)),
            pltpu.SemaphoreType.DMA((8, 2)),
        ],
        compiler_params=pltpu.CompilerParams(has_side_effects=True, vmem_limit_bytes=40 * 2**20),
        name="meet",
    )(panel, sizes, signs)


def place_kernel(blocks, front, tiles, out):
    group = lax.axis_index("group")
    member = lax.axis_index("member")
    half = pl.program_id(0)
    out[...] = front[...]
    run = 2 * group + half
    for g in range(8):
        for i in range(2):
            r = blocks[g, 2 * member + i] - SIDE * member
            for j in range(2):
                c = blocks[g, 2 * run + j] - SIDE * run
                where = (pl.ds(pl.multiple_of(r * B, B), B), pl.ds(pl.multiple_of(c * B, B), B))
                out[where] -= tiles[g, 0, i * B:(i + 1) * B, j * B:(j + 1) * B].astype(jnp.float32)


def place(blocks, front, tiles):
    return pl.pallas_call(
        place_kernel,
        grid=(2,),
        out_shape=jax.ShapeDtypeStruct(front.shape, jnp.float32),
        in_specs=[
            pl.BlockSpec(memory_space=pltpu.SMEM),
            pl.BlockSpec((512, 512), lambda h: (0, h)),
            pl.BlockSpec((8, 1, ROWS, ROWS), lambda h: (0, h, 0, 0)),
        ],
        out_specs=pl.BlockSpec((512, 512), lambda h: (0, h)),
        compiler_params=pltpu.CompilerParams(vmem_limit_bytes=32 * 2**20),
        name="place",
    )(blocks, front, tiles)


def local(root_front, child_panels, pivot_sizes, pivot_signs, child_blocks):
    tiles = meet(child_panels, pivot_sizes, pivot_signs)
    return place(child_blocks, root_front, tiles)


def solution(mesh):
    placed = (
        P("member", "group"),
        P("group", "member", None),
        P("group", None),
        P("group", None),
        P(),
    )
    return jax.shard_map(
        local, mesh=mesh, in_specs=placed, out_specs=P("member", "group"), check_vma=False
    )
```

```python
import jax
import jax.numpy as jnp
from jax import lax
from jax.experimental import pallas as pl
from jax.experimental.pallas import tpu as pltpu
from jax.sharding import PartitionSpec as P

B = 128
ROWS = 256
K = 4096
NC = 8
KC = K // NC
AHEAD = 3
SIDE = 4
pivot_floor = 0.1

TRI = ((0, 0), (0, 1), (1, 0), (1, 1), (0, 2), (2, 0))
PAIRS = (
    (0, 0, False),
    (0, 1, True),
    (0, 2, True),
    (2, 1, True),
    (0, 3, True),
    (0, 4, False),
    (2, 4, True),
    (0, 5, False),
    (5, 1, True),
    (5, 4, False),
)

TILES = tuple((n, a, b, False) for n, (a, b, _) in enumerate(PAIRS)) + tuple(
    (n, b, a, True) for n, (a, b, both) in enumerate(PAIRS) if both
)
NEAR, CORNER, FAR = (0, 1, 2, 3), (4,), (5, 6, 7, 8, 9)
PASS_NEAR, PASS_FAR = 3, 2


def dot_nt(left, right):
    return lax.dot_general(left, right, (((1,), (1,)), ((), ())), preferred_element_type=jnp.float32)


def meet_kernel(
    panel, sizes_in, signs_in, arrived, pan, sizes, signs, acc, stage, mine,
    load_sem, row_sem, hop_send, hop_recv, relay_send, relay_recv, tile_send, tile_recv,
):
    group = lax.axis_index("group")
    member = lax.axis_index("member")
    row, col = member // SIDE, member % SIDE
    turn = 1 - 2 * (group % 2)

    def at(offset):
        y = (row + turn * offset[0] + SIDE) % SIDE
        z = (col + turn * offset[1] + SIDE) % SIDE
        return y * SIDE + z

    to_z, to_y = at((0, -1)), at((-1, 0))

    def cols(k):
        return pl.ds(pl.multiple_of(k * KC, KC), KC)

    def load(k):
        return pltpu.make_async_copy(panel.at[0, :, cols(k)], pan.at[0, :, cols(k)], load_sem.at[k])

    load_sizes = pltpu.make_async_copy(sizes_in, sizes, row_sem.at[0])
    load_signs = pltpu.make_async_copy(signs_in, signs, row_sem.at[1])
    load_sizes.start()
    for k in range(NC):
        load(k).start()
    load_signs.start()

    barrier = pltpu.get_barrier_semaphore()

    def greet(g, m):
        pl.semaphore_signal(
            barrier, inc=1, device_id={"group": g, "member": m}, device_id_type=pl.DeviceIdType.MESH
        )

    greet(group, at((0, 1)))
    greet(group, at((1, 0)))
    for offset in TRI[1:]:
        greet(group, at((-offset[0], -offset[1])))
    for step in range(1, 8):
        greet((group + step) % 8, member)
    greeted = 2 + len(TRI[1:]) + 7

    def hop(src, dst, k, target):
        return pltpu.make_async_remote_copy(
            src_ref=pan.at[src, :, cols(k)],
            dst_ref=pan.at[dst, :, cols(k)],
            send_sem=hop_send.at[dst - 1, k],
            recv_sem=hop_recv.at[dst - 1, k],
            device_id={"group": group, "member": target},
            device_id_type=pl.DeviceIdType.MESH,
        )

    def hops_own(k):
        return hop(0, 1, k, to_z), hop(0, 2, k, to_y)

    def hops_far(k):
        return hop(1, 4, k, to_z), hop(2, 5, k, to_y)

    def hops_corner(c):
        return hop(2, 3, 2 * c, to_z), hop(1, 3, 2 * c + 1, to_y)

    def start(pair):
        for copy in pair:
            copy.start()

    def landed(pair):
        for copy in pair:
            copy.wait_recv()

    load_sizes.wait()
    root = jnp.sqrt(jnp.maximum(sizes[...], pivot_floor))
    for k in range(NC):
        load(k).wait()
        s = slice(k * KC, (k + 1) * KC)
        pan[0, :, s] = (pan[0, :, s].astype(jnp.float32) * root[:, s]).astype(jnp.bfloat16)
        if k == 0:
            pl.semaphore_wait(barrier, greeted)
        if k < AHEAD:
            start(hops_own(k))
    load_signs.wait()

    def signed(slot, k):
        s = (2 * signs[:, cols(k)] - 1).astype(jnp.float32).astype(jnp.bfloat16)
        return pan[slot, :, cols(k)] * s

    def accumulate(n, left, right, k):
        prod = dot_nt(left, pan[right, :, cols(k)])

        @pl.when(k == 0)
        def _():
            acc[n] = prod

        @pl.when(k > 0)
        def _():
            acc[n] += prod

    def relay(slot, r):
        return pltpu.make_async_remote_copy(
            src_ref=stage.at[slot],
            dst_ref=mine.at[slot],
            send_sem=relay_send.at[slot],
            recv_sem=relay_recv.at[slot],
            device_id={"group": group, "member": at(TRI[r])},
            device_id_type=pl.DeviceIdType.MESH,
        )

    def column_of(r, c):
        return at((TRI[c][0] - TRI[r][0], TRI[c][1] - TRI[r][1]))

    def deliver(slot, r, c):
        column = column_of(r, c)
        owner, half = column // 2, column % 2

        @pl.when(owner == group)
        def _():
            pltpu.make_async_copy(mine.at[slot], arrived.at[group, half], tile_recv.at[group, half]).start()

        @pl.when(owner != group)
        def _():
            remote_tile(slot, owner, half).start()

    def remote_tile(slot, owner, half):
        return pltpu.make_async_remote_copy(
            src_ref=mine.at[slot],
            dst_ref=arrived.at[group, half],
            send_sem=tile_send.at[slot],
            recv_sem=tile_recv.at[group, half],
            device_id={"group": owner, "member": member},
            device_id_type=pl.DeviceIdType.MESH,
        )

    def ship(pairs):
        for here in (False, True):
            for slot, (n, r, c, flipped) in enumerate(TILES):
                if n not in pairs or here != (r == 0):
                    continue
                value = acc[n].astype(jnp.bfloat16)
                value = value.T if flipped else value
                if here:
                    mine[slot] = value
                    deliver(slot, r, c)
                else:
                    stage[slot] = value
                    relay(slot, r).start()

    def pass_on(pairs):
        for slot, (n, r, c, _) in enumerate(TILES):
            if n in pairs and r != 0:
                relay(slot, r).wait_recv()
                deliver(slot, r, c)

    def near(k, carry):
        own = signed(0, k)
        accumulate(0, own, 0, k)
        landed(hops_own(k))

        @pl.when(k + AHEAD < NC)
        def _():
            start(hops_own(k + AHEAD))

        @pl.when(k + AHEAD >= NC)
        def _():
            start(hops_far(k + AHEAD - NC))

        accumulate(1, own, 1, k)
        accumulate(2, own, 2, k)
        accumulate(3, signed(2, k), 1, k)
        return carry

    lax.fori_loop(0, NC, near, 0)
    ship(NEAR)

    def far(k, carry):
        landed(hops_far(k))

        @pl.when(k + AHEAD < NC)
        def _():
            start(hops_far(k + AHEAD))

        @pl.when(k + AHEAD >= NC)
        def _():
            start(hops_corner(k + AHEAD - NC))

        @pl.when(k == PASS_NEAR)
        def _():
            pass_on(NEAR)

        own = signed(0, k)
        accumulate(5, own, 4, k)
        accumulate(6, signed(2, k), 4, k)
        accumulate(7, own, 5, k)
        last = signed(5, k)
        accumulate(8, last, 1, k)
        accumulate(9, last, 4, k)
        return carry

    lax.fori_loop(0, NC, far, 0)
    for c in range(AHEAD, NC // 2):
        start(hops_corner(c))
    ship(FAR)

    def corner(c, carry):
        landed(hops_corner(c))

        @pl.when(c == PASS_FAR)
        def _():
            pass_on(FAR)

        accumulate(4, signed(0, 2 * c), 3, 2 * c)
        accumulate(4, signed(0, 2 * c + 1), 3, 2 * c + 1)
        return carry

    lax.fori_loop(0, NC // 2, corner, 0)
    ship(CORNER)
    pass_on(CORNER)

    def drain(k, carry):
        for copy in hops_own(k) + hops_far(k):
            copy.wait_send()
        hop(2, 3, k, to_z).wait_send()
        return carry

    lax.fori_loop(0, NC, drain, 0)
    for slot, (_, r, c, _) in enumerate(TILES):
        if r != 0:
            relay(slot, r).wait_send()
        column = column_of(r, c)

        @pl.when(column // 2 != group)
        def _():
            remote_tile(slot, column // 2, column % 2).wait_send()

    for g in range(8):
        for j in range(2):
            pltpu.make_async_copy(stage.at[0], arrived.at[g, j], tile_recv.at[g, j]).wait()


def meet(panel, sizes, signs):
    return pl.pallas_call(
        meet_kernel,
        out_shape=jax.ShapeDtypeStruct((8, 2, ROWS, ROWS), jnp.bfloat16),
        in_specs=[pl.BlockSpec(memory_space=pltpu.HBM)] * 3,
        out_specs=pl.BlockSpec(memory_space=pl.ANY),
        scratch_shapes=[
            pltpu.VMEM((6, ROWS, K), jnp.bfloat16),
            pltpu.VMEM((1, K), jnp.float32),
            pltpu.VMEM((1, K), jnp.int32),
            pltpu.VMEM((10, ROWS, ROWS), jnp.float32),
            pltpu.VMEM((16, ROWS, ROWS), jnp.bfloat16),
            pltpu.VMEM((16, ROWS, ROWS), jnp.bfloat16),
            pltpu.SemaphoreType.DMA((NC,)),
            pltpu.SemaphoreType.DMA((2,)),
            pltpu.SemaphoreType.DMA((5, NC)),
            pltpu.SemaphoreType.DMA((5, NC)),
            pltpu.SemaphoreType.DMA((16,)),
            pltpu.SemaphoreType.DMA((16,)),
            pltpu.SemaphoreType.DMA((16,)),
            pltpu.SemaphoreType.DMA((8, 2)),
        ],
        compiler_params=pltpu.CompilerParams(
            collective_id=0, has_side_effects=True, vmem_limit_bytes=59 * 2**20
        ),
        name="meet",
    )(panel, sizes, signs)


def place_kernel(blocks, front, tiles, out):
    group = lax.axis_index("group")
    member = lax.axis_index("member")
    half = pl.program_id(0)
    out[...] = front[...]
    run = 2 * group + half
    for g in range(8):
        for i in range(2):
            r = blocks[g, 2 * member + i] - SIDE * member
            for j in range(2):
                c = blocks[g, 2 * run + j] - SIDE * run
                where = (pl.ds(pl.multiple_of(r * B, B), B), pl.ds(pl.multiple_of(c * B, B), B))
                out[where] -= tiles[g, 0, i * B:(i + 1) * B, j * B:(j + 1) * B].astype(jnp.float32)


def place(blocks, front, tiles):
    return pl.pallas_call(
        place_kernel,
        grid=(2,),
        out_shape=jax.ShapeDtypeStruct(front.shape, jnp.float32),
        in_specs=[
            pl.BlockSpec(memory_space=pltpu.SMEM),
            pl.BlockSpec((512, 512), lambda h: (0, h)),
            pl.BlockSpec((8, 1, ROWS, ROWS), lambda h: (0, h, 0, 0)),
        ],
        out_specs=pl.BlockSpec((512, 512), lambda h: (0, h)),
        compiler_params=pltpu.CompilerParams(vmem_limit_bytes=32 * 2**20),
        name="place",
    )(blocks, front, tiles)


def local(root_front, child_panels, pivot_sizes, pivot_signs, child_blocks):
    tiles = meet(child_panels, pivot_sizes, pivot_signs)
    return place(child_blocks, root_front, tiles)


def solution(mesh):
    placed = (
        P("member", "group"),
        P("group", "member", None),
        P("group", None),
        P("group", None),
        P(),
    )
    return jax.shard_map(
        local, mesh=mesh, in_specs=placed, out_specs=P("member", "group"), check_vma=False
    )
```

```python
import jax
import jax.numpy as jnp
from jax import lax
from jax.experimental import pallas as pl
from jax.experimental.pallas import tpu as pltpu
from jax.sharding import PartitionSpec as P

B = 128
ROWS = 256
K = 4096
NC = 8
KC = K // NC
KH = 2 * KC
AHEAD = 3
SIDE = 4
pivot_floor = 0.1

CROSS = ((0, 0), (0, 1), (1, 0), (0, 3), (0, 2), (2, 0))
PAIRS = (
    (0, 0), (0, 1), (0, 2), (2, 1),
    (0, 3), (2, 3), (5, 3),
    (0, 4), (2, 4), (0, 5), (1, 5),
    (4, 5),
)
TILES = tuple((n, a, b, False) for n, (a, b) in enumerate(PAIRS) if n != 6) + tuple(
    (n, PAIRS[n][1], PAIRS[n][0], True) for n in (2, 3, 5, 6, 8)
)
NEAR, CORNER, FAR, LAST = (0, 1, 2, 3), (4, 5, 6), (7, 8, 9, 10), (11,)
WHOLE = 2
PASS_NEAR, PASS_FAR, PASS_LAST = 2, 2, 2


def dot_nt(left, right):
    return lax.dot_general(left, right, (((1,), (1,)), ((), ())), preferred_element_type=jnp.float32)


def half_rows(h):
    return pl.ds(h * B if isinstance(h, int) else pl.multiple_of(h * B, B), B)


def part(ref, flipped, h):
    if h == WHOLE:
        return ref
    return ref.at[half_rows(h), :] if flipped else ref.at[:, half_rows(h)]


def meet_kernel(
    panel, sizes_in, signs_in, arrived, pan, sizes, signs, acc, stage, mine,
    load_sem, row_sem, hop_send, hop_recv, relay_send, relay_recv, tile_send, tile_recv,
):
    group = lax.axis_index("group")
    member = lax.axis_index("member")
    row, col = member // SIDE, member % SIDE
    odd = group % 2

    def at(offset):
        across, along = offset
        y = (row + jnp.where(odd == 0, across, -along) + SIDE) % SIDE
        z = (col + jnp.where(odd == 0, along, -across) + SIDE) % SIDE
        return y * SIDE + z

    to_back, to_across, to_ahead = at((0, -1)), at((-1, 0)), at((0, 1))

    def cols(k):
        return pl.ds(pl.multiple_of(k * KC, KC), KC)

    def load(k):
        return pltpu.make_async_copy(panel.at[0, :, cols(k)], pan.at[0, :, cols(k)], load_sem.at[k])

    load_sizes = pltpu.make_async_copy(sizes_in, sizes, row_sem.at[0])
    load_signs = pltpu.make_async_copy(signs_in, signs, row_sem.at[1])
    load_sizes.start()
    for k in range(NC):
        load(k).start()
    load_signs.start()

    barrier = pltpu.get_barrier_semaphore()

    def greet(g, m):
        pl.semaphore_signal(
            barrier, inc=1, device_id={"group": g, "member": m}, device_id_type=pl.DeviceIdType.MESH
        )

    for offset in ((0, 1), (1, 0), (0, -1)):
        greet(group, at(offset))
    rows_of = sorted({r for _, r, _, _ in TILES if r != 0})
    for r in rows_of:
        greet(group, at((-CROSS[r][0], -CROSS[r][1])))
    for step in range(1, 8):
        greet((group + step) % 8, member)
    greeted = 3 + len(rows_of) + 7

    def hop(src, dst, rows, columns, n, target):
        return pltpu.make_async_remote_copy(
            src_ref=pan.at[src, rows, columns],
            dst_ref=pan.at[dst, rows, columns],
            send_sem=hop_send.at[dst - 1, n],
            recv_sem=hop_recv.at[dst - 1, n],
            device_id={"group": group, "member": target},
            device_id_type=pl.DeviceIdType.MESH,
        )

    def wide(kk):
        return pl.ds(pl.multiple_of(kk * KH, KH), KH)

    def hops_own(k):
        return hop(0, 1, slice(None), cols(k), k, to_back), hop(0, 2, slice(None), cols(k), k, to_across)

    def hops_far(f):
        rows, columns = half_rows(f // 4), wide(f % 4)
        return hop(1, 4, rows, columns, f, to_back), hop(2, 5, rows, columns, f, to_across)

    def hops_corner(c):
        h, i = c // 2, c % 2
        return (
            hop(4, 3, half_rows(h), wide(i), 4 * h + i, to_back),
            hop(0, 3, half_rows(h), wide(2 + i), 4 * h + 2 + i, to_ahead),
        )

    def start(pair):
        for copy in pair:
            copy.start()

    def landed(pair):
        for copy in pair:
            copy.wait_recv()

    load_sizes.wait()
    root = jnp.sqrt(jnp.maximum(sizes[...], pivot_floor))
    for k in range(NC):
        load(k).wait()
        s = slice(k * KC, (k + 1) * KC)
        pan[0, :, s] = (pan[0, :, s].astype(jnp.float32) * root[:, s]).astype(jnp.bfloat16)
        if k == 0:
            pl.semaphore_wait(barrier, greeted)
        if k < AHEAD:
            start(hops_own(k))
    load_signs.wait()

    def signed(slot, rows, columns):
        s = (2 * signs[:, columns] - 1).astype(jnp.float32).astype(jnp.bfloat16)
        return pan[slot, rows, columns] * s

    def accumulate(n, rows, columns, prod, first):
        @pl.when(first)
        def _():
            acc[n, rows, columns] = prod

        @pl.when(jnp.logical_not(first))
        def _():
            acc[n, rows, columns] += prod

    def relay(slot, h):
        _, r, _, flipped = TILES[slot]
        return pltpu.make_async_remote_copy(
            src_ref=part(stage.at[slot], flipped, h),
            dst_ref=part(mine.at[slot], flipped, h),
            send_sem=relay_send.at[slot, h % 2],
            recv_sem=relay_recv.at[slot, h % 2],
            device_id={"group": group, "member": at(CROSS[r])},
            device_id_type=pl.DeviceIdType.MESH,
        )

    def home(slot):
        _, r, c, _ = TILES[slot]
        column = at((CROSS[c][0] - CROSS[r][0], CROSS[c][1] - CROSS[r][1]))
        return column // 2, column % 2

    def to_owner(slot, h):
        owner, side = home(slot)
        flipped = TILES[slot][3]
        return pltpu.make_async_remote_copy(
            src_ref=part(mine.at[slot], flipped, h),
            dst_ref=part(arrived.at[group, side], flipped, h),
            send_sem=tile_send.at[slot, h % 2],
            recv_sem=tile_recv.at[group, side],
            device_id={"group": owner, "member": member},
            device_id_type=pl.DeviceIdType.MESH,
        )

    def deliver(slot, h):
        owner, side = home(slot)
        flipped = TILES[slot][3]

        @pl.when(owner == group)
        def _():
            pltpu.make_async_copy(
                part(mine.at[slot], flipped, h),
                part(arrived.at[group, side], flipped, h),
                tile_recv.at[group, side],
            ).start()

        @pl.when(owner != group)
        def _():
            to_owner(slot, h).start()

    def ship(products, h):
        for here in (False, True):
            for slot, (n, r, _, flipped) in enumerate(TILES):
                if n not in products or here != (r == 0):
                    continue
                value = (acc[n] if h == WHOLE else acc[n, :, half_rows(h)]).astype(jnp.bfloat16)
                part((mine if here else stage).at[slot], flipped, h)[...] = value.T if flipped else value
                if here:
                    deliver(slot, h)
                else:
                    relay(slot, h).start()

    def pass_on(products, h):
        for slot, (n, r, _, _) in enumerate(TILES):
            if n in products and r != 0:
                relay(slot, h).wait_recv()
                deliver(slot, h)

    everything = slice(None)

    def near(k, carry):
        first = k == 0
        own = signed(0, everything, cols(k))
        accumulate(0, everything, everything, dot_nt(own, pan[0, :, cols(k)]), first)
        landed(hops_own(k))

        @pl.when(k + AHEAD < NC)
        def _():
            start(hops_own(k + AHEAD))

        @pl.when(k + AHEAD >= NC)
        def _():
            start(hops_far(k + AHEAD - NC))

        accumulate(1, everything, everything, dot_nt(own, pan[1, :, cols(k)]), first)
        accumulate(2, everything, everything, dot_nt(own, pan[2, :, cols(k)]), first)
        accumulate(3, everything, everything, dot_nt(signed(2, everything, cols(k)), pan[1, :, cols(k)]), first)
        return carry

    lax.fori_loop(0, NC, near, 0)
    ship(NEAR, WHOLE)

    def far(h, kk):
        f = 4 * h + kk
        landed(hops_far(f))

        @pl.when(f + AHEAD < NC)
        def _():
            start(hops_far(f + AHEAD))

        @pl.when(f + AHEAD >= NC)
        def _():
            start(hops_corner(f + AHEAD - NC))

        first = kk == 0
        here, where = half_rows(h), wide(kk)
        along = signed(4, here, where)
        accumulate(7, everything, here, dot_nt(pan[0, :, where], along), first)
        accumulate(8, everything, here, dot_nt(pan[2, :, where], along), first)
        across = signed(5, here, where)
        accumulate(9, everything, here, dot_nt(pan[0, :, where], across), first)
        accumulate(10, everything, here, dot_nt(pan[1, :, where], across), first)
        if h == 0:
            accumulate(11, here, here, dot_nt(pan[4, here, where], across), first)
        else:
            accumulate(11, everything, here, dot_nt(pan[4, :, where], across), first)
            accumulate(11, here, half_rows(0), dot_nt(along, pan[5, half_rows(0), where]), first)

    def far_first(kk, carry):
        far(0, kk)

        @pl.when(kk == PASS_NEAR)
        def _():
            pass_on(NEAR, WHOLE)

        return carry

    lax.fori_loop(0, 4, far_first, 0)
    ship(FAR, 0)

    def far_second(kk, carry):
        far(1, kk)

        @pl.when(kk == PASS_FAR)
        def _():
            pass_on(FAR, 0)

        return carry

    lax.fori_loop(0, 4, far_second, 0)
    for c in range(AHEAD, 4):
        start(hops_corner(c))
    ship(FAR, 1)
    ship(LAST, WHOLE)

    def corner(h, i):
        landed(hops_corner(2 * h + i))
        here = half_rows(h)
        low, high = signed(3, here, wide(i)), signed(3, here, wide(2 + i))
        for n in CORNER:
            left = PAIRS[n][0]
            prod = dot_nt(pan[left, :, wide(i)], low)
            prod += dot_nt(pan[left, :, wide(2 + i)], high)
            accumulate(n, everything, here, prod, i == 0)

    for h in range(2):
        for i in range(2):
            corner(h, i)
            if 2 * h + i == PASS_LAST:
                pass_on(FAR, 1)
                pass_on(LAST, WHOLE)
        ship(CORNER, h)
    pass_on(CORNER, 0)
    pass_on(CORNER, 1)

    def drain(k, carry):
        for copy in hops_own(k) + hops_far(k):
            copy.wait_send()
        return carry

    lax.fori_loop(0, NC, drain, 0)
    for c in range(4):
        for copy in hops_corner(c):
            copy.wait_send()
    for slot, (n, r, _, _) in enumerate(TILES):
        for h in (WHOLE,) if n in NEAR + LAST else (0, 1):
            if r != 0:
                relay(slot, h).wait_send()

            @pl.when(home(slot)[0] != group)
            def _():
                to_owner(slot, h).wait_send()

    for g in range(8):
        for j in range(2):
            pltpu.make_async_copy(mine.at[0], arrived.at[g, j], tile_recv.at[g, j]).wait()


def meet(panel, sizes, signs):
    return pl.pallas_call(
        meet_kernel,
        out_shape=jax.ShapeDtypeStruct((8, 2, ROWS, ROWS), jnp.bfloat16),
        in_specs=[pl.BlockSpec(memory_space=pltpu.HBM)] * 3,
        out_specs=pl.BlockSpec(memory_space=pl.ANY),
        scratch_shapes=[
            pltpu.VMEM((6, ROWS, K), jnp.bfloat16),
            pltpu.VMEM((1, K), jnp.float32),
            pltpu.VMEM((1, K), jnp.int32),
            pltpu.VMEM((12, ROWS, ROWS), jnp.float32),
            pltpu.VMEM((16, ROWS, ROWS), jnp.bfloat16),
            pltpu.VMEM((16, ROWS, ROWS), jnp.bfloat16),
            pltpu.SemaphoreType.DMA((NC,)),
            pltpu.SemaphoreType.DMA((2,)),
            pltpu.SemaphoreType.DMA((5, NC)),
            pltpu.SemaphoreType.DMA((5, NC)),
            pltpu.SemaphoreType.DMA((16, 2)),
            pltpu.SemaphoreType.DMA((16, 2)),
            pltpu.SemaphoreType.DMA((16, 2)),
            pltpu.SemaphoreType.DMA((8, 2)),
        ],
        compiler_params=pltpu.CompilerParams(
            collective_id=0, has_side_effects=True, vmem_limit_bytes=59 * 2**20
        ),
        name="meet",
    )(panel, sizes, signs)


def place_kernel(blocks_in, front, tiles_in, out, blocks, total, tiles, blocks_sem, front_sem, tiles_sem, out_sem):
    group = lax.axis_index("group")
    member = lax.axis_index("member")
    width = 4 * B

    def load_front(j):
        return pltpu.make_async_copy(
            front.at[:, j * width:(j + 1) * width], total.at[:, j * width:(j + 1) * width], front_sem.at[j]
        )

    def load_tile(g, j):
        return pltpu.make_async_copy(tiles_in.at[g, j], tiles.at[g, j], tiles_sem.at[g, j])

    def store(j):
        return pltpu.make_async_copy(
            total.at[:, j * width:(j + 1) * width], out.at[:, j * width:(j + 1) * width], out_sem.at[j]
        )

    load_blocks = pltpu.make_async_copy(blocks_in, blocks, blocks_sem)
    load_blocks.start()
    for j in range(2):
        load_front(j).start()
        for g in range(8):
            load_tile(g, j).start()
    load_blocks.wait()
    for j in range(2):
        run = 2 * group + j
        load_front(j).wait()
        for g in range(8):
            load_tile(g, j).wait()
            for a in range(2):
                r = blocks[g, 2 * member + a] - SIDE * member
                for b in range(2):
                    c = blocks[g, 2 * run + b] - SIDE * run + SIDE * j
                    where = (pl.ds(pl.multiple_of(r * B, B), B), pl.ds(pl.multiple_of(c * B, B), B))
                    total[where] -= tiles[g, j, a * B:(a + 1) * B, b * B:(b + 1) * B].astype(jnp.float32)
        store(j).start()
    for j in range(2):
        store(j).wait()


def place(blocks, front, tiles):
    return pl.pallas_call(
        place_kernel,
        out_shape=jax.ShapeDtypeStruct(front.shape, jnp.float32),
        in_specs=[pl.BlockSpec(memory_space=pl.ANY)] * 3,
        out_specs=pl.BlockSpec(memory_space=pl.ANY),
        scratch_shapes=[
            pltpu.SMEM(blocks.shape, jnp.int32),
            pltpu.VMEM(front.shape, jnp.float32),
            pltpu.VMEM(tiles.shape, jnp.bfloat16),
            pltpu.SemaphoreType.DMA,
            pltpu.SemaphoreType.DMA((2,)),
            pltpu.SemaphoreType.DMA((8, 2)),
            pltpu.SemaphoreType.DMA((2,)),
        ],
        compiler_params=pltpu.CompilerParams(vmem_limit_bytes=62 * 2**20),
        name="place",
    )(blocks, front, tiles)


def local(root_front, child_panels, pivot_sizes, pivot_signs, child_blocks):
    tiles = meet(child_panels, pivot_sizes, pivot_signs)
    return place(child_blocks, root_front, tiles)


def solution(mesh):
    placed = (
        P("member", "group"),
        P("group", "member", None),
        P("group", None),
        P("group", None),
        P(),
    )
    return jax.shard_map(
        local, mesh=mesh, in_specs=placed, out_specs=P("member", "group"), check_vma=False
    )
```

```python
import jax
import jax.numpy as jnp
from jax import lax
from jax.experimental import pallas as pl
from jax.experimental.pallas import tpu as pltpu
from jax.sharding import PartitionSpec as P

B = 128
ROWS = 256
K = 4096
NC = 8
KC = K // NC
KH = 2 * KC
AHEAD = 3
SIDE = 4
pivot_floor = 0.1

CROSS = ((0, 0), (0, 1), (1, 0), (0, 3), (0, 2), (2, 0))
PAIRS = (
    (0, 0), (0, 1), (0, 2), (2, 1),
    (0, 3), (2, 3), (5, 3),
    (0, 4), (2, 4), (0, 5), (1, 5),
    (4, 5),
)
TILES = tuple((n, a, b, False) for n, (a, b) in enumerate(PAIRS) if n != 6) + tuple(
    (n, PAIRS[n][1], PAIRS[n][0], True) for n in (2, 3, 5, 6, 8)
)
NEAR, CORNER, FAR, LAST = (0, 1, 2, 3), (4, 5, 6), (7, 8, 9, 10), (11,)
WHOLE = 2
PASS_NEAR, PASS_FAR = 2, 2
EARLY = 2


def dot_nt(left, right):
    return lax.dot_general(left, right, (((1,), (1,)), ((), ())), preferred_element_type=jnp.float32)


def half_rows(h):
    return pl.ds(h * B if isinstance(h, int) else pl.multiple_of(h * B, B), B)


def part(ref, flipped, h):
    if h == WHOLE:
        return ref
    return ref.at[half_rows(h), :] if flipped else ref.at[:, half_rows(h)]


def meet_kernel(
    panel, sizes_in, signs_in, arrived, pan, sizes, signs, acc, stage, mine,
    load_sem, row_sem, hop_send, hop_recv, relay_send, relay_recv, tile_send, tile_recv,
):
    group = lax.axis_index("group")
    member = lax.axis_index("member")
    row, col = member // SIDE, member % SIDE
    odd = group % 2

    def at(offset):
        across, along = offset
        y = (row + jnp.where(odd == 0, across, -along) + SIDE) % SIDE
        z = (col + jnp.where(odd == 0, along, -across) + SIDE) % SIDE
        return y * SIDE + z

    to_back, to_across, to_ahead = at((0, -1)), at((-1, 0)), at((0, 1))

    def cols(k):
        return pl.ds(pl.multiple_of(k * KC, KC), KC)

    def load(k):
        return pltpu.make_async_copy(panel.at[0, :, cols(k)], pan.at[0, :, cols(k)], load_sem.at[k])

    load_sizes = pltpu.make_async_copy(sizes_in, sizes, row_sem.at[0])
    load_signs = pltpu.make_async_copy(signs_in, signs, row_sem.at[1])
    load_sizes.start()
    for k in range(NC):
        load(k).start()
    load_signs.start()

    barrier = pltpu.get_barrier_semaphore()

    def greet(g, m):
        pl.semaphore_signal(
            barrier, inc=1, device_id={"group": g, "member": m}, device_id_type=pl.DeviceIdType.MESH
        )

    for offset in ((0, 1), (1, 0), (0, -1)):
        greet(group, at(offset))
    rows_of = sorted({r for _, r, _, _ in TILES if r != 0})
    for r in rows_of:
        greet(group, at((-CROSS[r][0], -CROSS[r][1])))
    for step in range(1, 8):
        greet((group + step) % 8, member)
    greeted = 3 + len(rows_of) + 7

    def hop(src, dst, rows, columns, n, target):
        return pltpu.make_async_remote_copy(
            src_ref=pan.at[src, rows, columns],
            dst_ref=pan.at[dst, rows, columns],
            send_sem=hop_send.at[dst - 1, n],
            recv_sem=hop_recv.at[dst - 1, n],
            device_id={"group": group, "member": target},
            device_id_type=pl.DeviceIdType.MESH,
        )

    def wide(kk):
        return pl.ds(pl.multiple_of(kk * KH, KH), KH)

    def hops_own(k):
        return hop(0, 1, slice(None), cols(k), k, to_back), hop(0, 2, slice(None), cols(k), k, to_across)

    def hops_far(f):
        rows, columns = half_rows(f // 4), wide(f % 4)
        return hop(1, 4, rows, columns, f, to_back), hop(2, 5, rows, columns, f, to_across)

    def hops_corner(c):
        h, i = c // 2, c % 2
        return (
            hop(4, 3, half_rows(h), wide(i), 4 * h + i, to_back),
            hop(0, 3, half_rows(h), wide(2 + i), 4 * h + 2 + i, to_ahead),
        )

    def start(pair):
        for copy in pair:
            copy.start()

    def landed(pair):
        for copy in pair:
            copy.wait_recv()

    load_sizes.wait()
    root = jnp.sqrt(jnp.maximum(sizes[...], pivot_floor))
    for k in range(NC):
        load(k).wait()
        s = slice(k * KC, (k + 1) * KC)
        pan[0, :, s] = (pan[0, :, s].astype(jnp.float32) * root[:, s]).astype(jnp.bfloat16)
        if k == 0:
            pl.semaphore_wait(barrier, greeted)
        if k < AHEAD:
            start(hops_own(k))
    load_signs.wait()
    acc[...] = jnp.zeros_like(acc)

    def signed(slot, rows, columns):
        s = (2 * signs[:, columns] - 1).astype(jnp.float32).astype(jnp.bfloat16)
        return pan[slot, rows, columns] * s

    def accumulate(n, rows, columns, prod):
        acc[n, rows, columns] += prod

    def relay(slot, h):
        _, r, _, flipped = TILES[slot]
        return pltpu.make_async_remote_copy(
            src_ref=part(stage.at[slot], flipped, h),
            dst_ref=part(mine.at[slot], flipped, h),
            send_sem=relay_send.at[slot, h % 2],
            recv_sem=relay_recv.at[slot, h % 2],
            device_id={"group": group, "member": at(CROSS[r])},
            device_id_type=pl.DeviceIdType.MESH,
        )

    def home(slot):
        _, r, c, _ = TILES[slot]
        column = at((CROSS[c][0] - CROSS[r][0], CROSS[c][1] - CROSS[r][1]))
        return column // 2, column % 2

    def to_owner(slot, h):
        owner, side = home(slot)
        flipped = TILES[slot][3]
        return pltpu.make_async_remote_copy(
            src_ref=part(mine.at[slot], flipped, h),
            dst_ref=part(arrived.at[group, side], flipped, h),
            send_sem=tile_send.at[slot, h % 2],
            recv_sem=tile_recv.at[group, side],
            device_id={"group": owner, "member": member},
            device_id_type=pl.DeviceIdType.MESH,
        )

    def deliver(slot, h):
        owner, side = home(slot)
        flipped = TILES[slot][3]

        @pl.when(owner == group)
        def _():
            pltpu.make_async_copy(
                part(mine.at[slot], flipped, h),
                part(arrived.at[group, side], flipped, h),
                tile_recv.at[group, side],
            ).start()

        @pl.when(owner != group)
        def _():
            to_owner(slot, h).start()

    def ship(products, h):
        for here in (False, True):
            for slot, (n, r, _, flipped) in enumerate(TILES):
                if n not in products or here != (r == 0):
                    continue
                value = (acc[n] if h == WHOLE else acc[n, :, half_rows(h)]).astype(jnp.bfloat16)
                part((mine if here else stage).at[slot], flipped, h)[...] = value.T if flipped else value
                if here:
                    deliver(slot, h)
                else:
                    relay(slot, h).start()

    def pass_on(products, h):
        for slot, (n, r, _, _) in enumerate(TILES):
            if n in products and r != 0:
                relay(slot, h).wait_recv()
                deliver(slot, h)

    everything = slice(None)

    def near(k, carry):
        own = signed(0, everything, cols(k))
        accumulate(0, everything, everything, dot_nt(own, pan[0, :, cols(k)]))
        landed(hops_own(k))

        @pl.when(k + AHEAD < NC)
        def _():
            start(hops_own(k + AHEAD))

        @pl.when(k + AHEAD >= NC)
        def _():
            start(hops_far(k + AHEAD - NC))

        accumulate(1, everything, everything, dot_nt(own, pan[1, :, cols(k)]))
        accumulate(2, everything, everything, dot_nt(own, pan[2, :, cols(k)]))
        accumulate(3, everything, everything, dot_nt(signed(2, everything, cols(k)), pan[1, :, cols(k)]))
        return carry

    lax.fori_loop(0, NC, near, 0)
    ship(NEAR, WHOLE)

    def far(h, kk):
        f = 4 * h + kk
        landed(hops_far(f))

        @pl.when(f + AHEAD < NC)
        def _():
            start(hops_far(f + AHEAD))

        @pl.when(jnp.logical_and(f + AHEAD >= NC, f + AHEAD < NC + EARLY))
        def _():
            start(hops_corner(f + AHEAD - NC))

        here, where = half_rows(h), wide(kk)
        along = signed(4, here, where)
        accumulate(7, everything, here, dot_nt(pan[0, :, where], along))
        accumulate(8, everything, here, dot_nt(pan[2, :, where], along))
        across = signed(5, here, where)
        accumulate(9, everything, here, dot_nt(pan[0, :, where], across))
        accumulate(10, everything, here, dot_nt(pan[1, :, where], across))
        if h == 0:
            accumulate(11, here, here, dot_nt(pan[4, here, where], across))
        else:
            accumulate(11, everything, here, dot_nt(pan[4, :, where], across))
            accumulate(11, here, half_rows(0), dot_nt(along, pan[5, half_rows(0), where]))

    def far_first(kk, carry):
        far(0, kk)

        @pl.when(kk == PASS_NEAR)
        def _():
            pass_on(NEAR, WHOLE)

        return carry

    lax.fori_loop(0, 4, far_first, 0)
    ship(FAR, 0)

    def far_second(kk, carry):
        far(1, kk)

        @pl.when(kk == PASS_FAR)
        def _():
            pass_on(FAR, 0)

        return carry

    lax.fori_loop(0, 4, far_second, 0)
    ship(FAR, 1)
    ship(LAST, WHOLE)
    for c in range(EARLY, 4):
        start(hops_corner(c))

    def corner(h, i):
        landed(hops_corner(2 * h + i))
        here = half_rows(h)
        low, high = signed(3, here, wide(i)), signed(3, here, wide(2 + i))
        for n in CORNER:
            left = PAIRS[n][0]
            prod = dot_nt(pan[left, :, wide(i)], low)
            prod += dot_nt(pan[left, :, wide(2 + i)], high)
            accumulate(n, everything, here, prod)

    corner(0, 0)
    corner(0, 1)
    ship(CORNER, 0)
    pass_on(FAR, 1)
    pass_on(LAST, WHOLE)
    corner(1, 0)
    corner(1, 1)
    pass_on(CORNER, 0)
    ship(CORNER, 1)
    pass_on(CORNER, 1)

    def drain(k, carry):
        for copy in hops_own(k) + hops_far(k):
            copy.wait_send()
        return carry

    lax.fori_loop(0, NC, drain, 0)
    for c in range(4):
        for copy in hops_corner(c):
            copy.wait_send()
    for slot, (n, r, _, _) in enumerate(TILES):
        for h in (WHOLE,) if n in NEAR + LAST else (0, 1):
            if r != 0:
                relay(slot, h).wait_send()

            @pl.when(home(slot)[0] != group)
            def _():
                to_owner(slot, h).wait_send()

    for g in range(8):
        for j in range(2):
            pltpu.make_async_copy(mine.at[0], arrived.at[g, j], tile_recv.at[g, j]).wait()


def meet(panel, sizes, signs):
    return pl.pallas_call(
        meet_kernel,
        out_shape=jax.ShapeDtypeStruct((8, 2, ROWS, ROWS), jnp.bfloat16),
        in_specs=[pl.BlockSpec(memory_space=pltpu.HBM)] * 3,
        out_specs=pl.BlockSpec(memory_space=pl.ANY),
        scratch_shapes=[
            pltpu.VMEM((6, ROWS, K), jnp.bfloat16),
            pltpu.VMEM((1, K), jnp.float32),
            pltpu.VMEM((1, K), jnp.int32),
            pltpu.VMEM((12, ROWS, ROWS), jnp.float32),
            pltpu.VMEM((16, ROWS, ROWS), jnp.bfloat16),
            pltpu.VMEM((16, ROWS, ROWS), jnp.bfloat16),
            pltpu.SemaphoreType.DMA((NC,)),
            pltpu.SemaphoreType.DMA((2,)),
            pltpu.SemaphoreType.DMA((5, NC)),
            pltpu.SemaphoreType.DMA((5, NC)),
            pltpu.SemaphoreType.DMA((16, 2)),
            pltpu.SemaphoreType.DMA((16, 2)),
            pltpu.SemaphoreType.DMA((16, 2)),
            pltpu.SemaphoreType.DMA((8, 2)),
        ],
        compiler_params=pltpu.CompilerParams(
            collective_id=0, has_side_effects=True, vmem_limit_bytes=40 * 2**20
        ),
        name="meet",
    )(panel, sizes, signs)


def place_kernel(blocks, front, tiles, out, total, out_sem):
    group = lax.axis_index("group")
    member = lax.axis_index("member")
    width = 4 * B

    def store(j):
        return pltpu.make_async_copy(
            total.at[:, j * width:(j + 1) * width], out.at[:, j * width:(j + 1) * width], out_sem.at[j]
        )

    for j in range(2):
        run = 2 * group + j
        side = slice(j * width, (j + 1) * width)
        total[:, side] = front[:, side]
        for g in range(8):
            for a in range(2):
                r = blocks[g, 2 * member + a] - SIDE * member
                for b in range(2):
                    c = blocks[g, 2 * run + b] - SIDE * run + SIDE * j
                    where = (pl.ds(pl.multiple_of(r * B, B), B), pl.ds(pl.multiple_of(c * B, B), B))
                    total[where] -= tiles[g, j, a * B:(a + 1) * B, b * B:(b + 1) * B].astype(jnp.float32)
        store(j).start()
    for j in range(2):
        store(j).wait()


def place(blocks, front, tiles):
    return pl.pallas_call(
        place_kernel,
        out_shape=jax.ShapeDtypeStruct(front.shape, jnp.float32),
        in_specs=[
            pl.BlockSpec(memory_space=pltpu.SMEM),
            pl.BlockSpec(memory_space=pltpu.VMEM),
            pl.BlockSpec(memory_space=pltpu.VMEM),
        ],
        out_specs=pl.BlockSpec(memory_space=pl.ANY),
        scratch_shapes=[
            pltpu.VMEM(front.shape, jnp.float32),
            pltpu.SemaphoreType.DMA((2,)),
        ],
        compiler_params=pltpu.CompilerParams(vmem_limit_bytes=32 * 2**20),
        name="place",
    )(blocks, front, tiles)


def local(root_front, child_panels, pivot_sizes, pivot_signs, child_blocks):
    kept = [pltpu.with_memory_space_constraint(x, pltpu.HBM) for x in (child_panels, pivot_sizes, pivot_signs)]
    tiles = meet(*kept)
    return place(child_blocks, root_front, tiles)


def solution(mesh):
    placed = (
        P("member", "group"),
        P("group", "member", None),
        P("group", None),
        P("group", None),
        P(),
    )
    return jax.shard_map(
        local, mesh=mesh, in_specs=placed, out_specs=P("member", "group"), check_vma=False
    )
```

```python
import jax
import jax.numpy as jnp
from jax import lax
from jax.experimental import pallas as pl
from jax.experimental.pallas import tpu as pltpu
from jax.sharding import PartitionSpec as P

B = 128
ROWS = 256
K = 4096
NC = 8
KC = K // NC
KH = 2 * KC
AHEAD = 3
SIDE = 4
pivot_floor = 0.1

CROSS = ((0, 0), (0, 1), (1, 0), (0, 3), (0, 2), (2, 0))
PAIRS = (
    (0, 0), (0, 1), (0, 2), (2, 1),
    (0, 3), (2, 3), (5, 3),
    (0, 4), (2, 4), (0, 5), (1, 5),
    (4, 5),
)
TILES = tuple((n, a, b, False) for n, (a, b) in enumerate(PAIRS) if n != 6) + tuple(
    (n, PAIRS[n][1], PAIRS[n][0], True) for n in (2, 3, 5, 6, 8)
)
SELF, NEAR, CORNER, FAR, LAST = (0,), (1, 2, 3), (4, 5, 6), (7, 8, 9, 10), (11,)
WHOLE = 2
PASS_NEAR, PASS_FAR = 2, 2
EARLY = 3


def dot_nt(left, right):
    return lax.dot_general(left, right, (((1,), (1,)), ((), ())), preferred_element_type=jnp.float32)


def half_rows(h):
    return pl.ds(h * B if isinstance(h, int) else pl.multiple_of(h * B, B), B)


def part(ref, flipped, h):
    if h == WHOLE:
        return ref
    return ref.at[half_rows(h), :] if flipped else ref.at[:, half_rows(h)]


def meet_kernel(
    panel, sizes_in, signs_in, arrived, pan, sizes, signs, acc, stage, mine,
    load_sem, row_sem, hop_send, hop_recv, relay_send, relay_recv, tile_send, tile_recv,
):
    group = lax.axis_index("group")
    member = lax.axis_index("member")
    row, col = member // SIDE, member % SIDE
    odd = group % 2

    def at(offset):
        across, along = offset
        y = (row + jnp.where(odd == 0, across, -along) + SIDE) % SIDE
        z = (col + jnp.where(odd == 0, along, -across) + SIDE) % SIDE
        return y * SIDE + z

    to_back, to_across, to_ahead = at((0, -1)), at((-1, 0)), at((0, 1))

    def cols(k):
        return pl.ds(pl.multiple_of(k * KC, KC), KC)

    def load(k):
        return pltpu.make_async_copy(panel.at[0, :, cols(k)], pan.at[0, :, cols(k)], load_sem.at[k])

    load_sizes = pltpu.make_async_copy(sizes_in, sizes, row_sem.at[0])
    load_signs = pltpu.make_async_copy(signs_in, signs, row_sem.at[1])
    load_sizes.start()
    for k in range(NC):
        load(k).start()
    load_signs.start()

    barrier = pltpu.get_barrier_semaphore()

    def greet(g, m):
        pl.semaphore_signal(
            barrier, inc=1, device_id={"group": g, "member": m}, device_id_type=pl.DeviceIdType.MESH
        )

    for offset in ((0, 1), (1, 0), (0, -1)):
        greet(group, at(offset))
    rows_of = sorted({r for _, r, _, _ in TILES if r != 0})
    for r in rows_of:
        greet(group, at((-CROSS[r][0], -CROSS[r][1])))
    for step in range(1, 8):
        greet((group + step) % 8, member)
    greeted = 3 + len(rows_of) + 7

    def hop(src, dst, rows, columns, n, target):
        return pltpu.make_async_remote_copy(
            src_ref=pan.at[src, rows, columns],
            dst_ref=pan.at[dst, rows, columns],
            send_sem=hop_send.at[dst - 1, n],
            recv_sem=hop_recv.at[dst - 1, n],
            device_id={"group": group, "member": target},
            device_id_type=pl.DeviceIdType.MESH,
        )

    def wide(kk):
        return pl.ds(pl.multiple_of(kk * KH, KH), KH)

    def hops_own(k):
        return hop(0, 1, slice(None), cols(k), k, to_back), hop(0, 2, slice(None), cols(k), k, to_across)

    def hops_far(f):
        rows, columns = half_rows(f // 4), wide(f % 4)
        return hop(1, 4, rows, columns, f, to_back), hop(2, 5, rows, columns, f, to_across)

    def hops_corner(c):
        h, i = c // 2, c % 2
        return (
            hop(4, 3, half_rows(h), wide(i), 4 * h + i, to_back),
            hop(0, 3, half_rows(h), wide(2 + i), 4 * h + 2 + i, to_ahead),
        )

    def start(pair):
        for copy in pair:
            copy.start()

    def landed(pair):
        for copy in pair:
            copy.wait_recv()

    load_sizes.wait()
    root = jnp.sqrt(jnp.maximum(sizes[...], pivot_floor))
    for k in range(NC):
        load(k).wait()
        s = slice(k * KC, (k + 1) * KC)
        pan[0, :, s] = (pan[0, :, s].astype(jnp.float32) * root[:, s]).astype(jnp.bfloat16)
        if k == 0:
            pl.semaphore_wait(barrier, greeted)
        if k < AHEAD:
            start(hops_own(k))
    load_signs.wait()
    acc[...] = jnp.zeros_like(acc)

    def signed(slot, rows, columns):
        s = (2 * signs[:, columns] - 1).astype(jnp.float32).astype(jnp.bfloat16)
        return pan[slot, rows, columns] * s

    def accumulate(n, rows, columns, prod):
        acc[n, rows, columns] += prod

    def relay(slot, h):
        _, r, _, flipped = TILES[slot]
        return pltpu.make_async_remote_copy(
            src_ref=part(stage.at[slot], flipped, h),
            dst_ref=part(mine.at[slot], flipped, h),
            send_sem=relay_send.at[slot, h % 2],
            recv_sem=relay_recv.at[slot, h % 2],
            device_id={"group": group, "member": at(CROSS[r])},
            device_id_type=pl.DeviceIdType.MESH,
        )

    def home(slot):
        _, r, c, _ = TILES[slot]
        column = at((CROSS[c][0] - CROSS[r][0], CROSS[c][1] - CROSS[r][1]))
        return column // 2, column % 2

    def to_owner(slot, h):
        owner, side = home(slot)
        flipped = TILES[slot][3]
        return pltpu.make_async_remote_copy(
            src_ref=part(mine.at[slot], flipped, h),
            dst_ref=part(arrived.at[group, side], flipped, h),
            send_sem=tile_send.at[slot, h % 2],
            recv_sem=tile_recv.at[group, side],
            device_id={"group": owner, "member": member},
            device_id_type=pl.DeviceIdType.MESH,
        )

    def deliver(slot, h):
        owner, side = home(slot)
        flipped = TILES[slot][3]

        @pl.when(owner == group)
        def _():
            pltpu.make_async_copy(
                part(mine.at[slot], flipped, h),
                part(arrived.at[group, side], flipped, h),
                tile_recv.at[group, side],
            ).start()

        @pl.when(owner != group)
        def _():
            to_owner(slot, h).start()

    def ship(products, h):
        for here in (False, True):
            for slot, (n, r, _, flipped) in enumerate(TILES):
                if n not in products or here != (r == 0):
                    continue
                value = (acc[n] if h == WHOLE else acc[n, :, half_rows(h)]).astype(jnp.bfloat16)
                part((mine if here else stage).at[slot], flipped, h)[...] = value.T if flipped else value
                if here:
                    deliver(slot, h)
                else:
                    relay(slot, h).start()

    def pass_on(products, h):
        for slot, (n, r, _, _) in enumerate(TILES):
            if n in products and r != 0:
                relay(slot, h).wait_recv()
                deliver(slot, h)

    everything = slice(None)

    def near(k, carry):
        own = signed(0, everything, cols(k))
        landed(hops_own(k))

        @pl.when(k + AHEAD < NC)
        def _():
            start(hops_own(k + AHEAD))

        @pl.when(k + AHEAD >= NC)
        def _():
            start(hops_far(k + AHEAD - NC))

        accumulate(1, everything, everything, dot_nt(own, pan[1, :, cols(k)]))
        accumulate(2, everything, everything, dot_nt(own, pan[2, :, cols(k)]))
        accumulate(3, everything, everything, dot_nt(signed(2, everything, cols(k)), pan[1, :, cols(k)]))
        return carry

    def self_product(k, carry):
        accumulate(0, everything, everything, dot_nt(signed(0, everything, cols(k)), pan[0, :, cols(k)]))
        return carry

    lax.fori_loop(0, NC, self_product, 0)
    ship(SELF, WHOLE)
    lax.fori_loop(0, NC, near, 0)
    ship(NEAR, WHOLE)

    def far(h, kk):
        f = 4 * h + kk
        landed(hops_far(f))

        @pl.when(f + AHEAD < NC)
        def _():
            start(hops_far(f + AHEAD))

        @pl.when(jnp.logical_and(f + AHEAD >= NC, f + AHEAD < NC + EARLY))
        def _():
            start(hops_corner(f + AHEAD - NC))

        here, where = half_rows(h), wide(kk)
        along = signed(4, here, where)
        accumulate(7, everything, here, dot_nt(pan[0, :, where], along))
        accumulate(8, everything, here, dot_nt(pan[2, :, where], along))
        across = signed(5, here, where)
        accumulate(9, everything, here, dot_nt(pan[0, :, where], across))
        accumulate(10, everything, here, dot_nt(pan[1, :, where], across))
        if h == 0:
            accumulate(11, here, here, dot_nt(pan[4, here, where], across))
        else:
            accumulate(11, everything, here, dot_nt(pan[4, :, where], across))
            accumulate(11, here, half_rows(0), dot_nt(along, pan[5, half_rows(0), where]))

    def far_first(kk, carry):
        far(0, kk)

        @pl.when(kk == PASS_NEAR)
        def _():
            pass_on(NEAR, WHOLE)

        return carry

    lax.fori_loop(0, 4, far_first, 0)
    ship(FAR, 0)

    def far_second(kk, carry):
        far(1, kk)

        @pl.when(kk == PASS_FAR)
        def _():
            pass_on(FAR, 0)

        return carry

    lax.fori_loop(0, 4, far_second, 0)
    ship(FAR, 1)
    ship(LAST, WHOLE)
    for c in range(EARLY, 4):
        start(hops_corner(c))

    def corner(h, i):
        landed(hops_corner(2 * h + i))
        here = half_rows(h)
        low, high = signed(3, here, wide(i)), signed(3, here, wide(2 + i))
        for n in CORNER:
            left = PAIRS[n][0]
            prod = dot_nt(pan[left, :, wide(i)], low)
            prod += dot_nt(pan[left, :, wide(2 + i)], high)
            accumulate(n, everything, here, prod)

    corner(0, 0)
    corner(0, 1)
    ship(CORNER, 0)
    pass_on(FAR, 1)
    pass_on(LAST, WHOLE)
    corner(1, 0)
    corner(1, 1)
    pass_on(CORNER, 0)
    ship(CORNER, 1)
    pass_on(CORNER, 1)

    def drain(k, carry):
        for copy in hops_own(k) + hops_far(k):
            copy.wait_send()
        return carry

    lax.fori_loop(0, NC, drain, 0)
    for c in range(4):
        for copy in hops_corner(c):
            copy.wait_send()
    for slot, (n, r, _, _) in enumerate(TILES):
        for h in (WHOLE,) if n in SELF + NEAR + LAST else (0, 1):
            if r != 0:
                relay(slot, h).wait_send()

            @pl.when(home(slot)[0] != group)
            def _():
                to_owner(slot, h).wait_send()

    for g in range(8):
        for j in range(2):
            pltpu.make_async_copy(mine.at[0], arrived.at[g, j], tile_recv.at[g, j]).wait()


def meet(panel, sizes, signs):
    return pl.pallas_call(
        meet_kernel,
        out_shape=jax.ShapeDtypeStruct((8, 2, ROWS, ROWS), jnp.bfloat16),
        in_specs=[pl.BlockSpec(memory_space=pltpu.HBM)] * 3,
        out_specs=pl.BlockSpec(memory_space=pl.ANY),
        scratch_shapes=[
            pltpu.VMEM((6, ROWS, K), jnp.bfloat16),
            pltpu.VMEM((1, K), jnp.float32),
            pltpu.VMEM((1, K), jnp.int32),
            pltpu.VMEM((12, ROWS, ROWS), jnp.float32),
            pltpu.VMEM((16, ROWS, ROWS), jnp.bfloat16),
            pltpu.VMEM((16, ROWS, ROWS), jnp.bfloat16),
            pltpu.SemaphoreType.DMA((NC,)),
            pltpu.SemaphoreType.DMA((2,)),
            pltpu.SemaphoreType.DMA((5, NC)),
            pltpu.SemaphoreType.DMA((5, NC)),
            pltpu.SemaphoreType.DMA((16, 2)),
            pltpu.SemaphoreType.DMA((16, 2)),
            pltpu.SemaphoreType.DMA((16, 2)),
            pltpu.SemaphoreType.DMA((8, 2)),
        ],
        compiler_params=pltpu.CompilerParams(
            collective_id=0, has_side_effects=True, vmem_limit_bytes=40 * 2**20
        ),
        name="meet",
    )(panel, sizes, signs)


def place_kernel(blocks_in, front, tiles, out, blocks, total, blocks_sem, out_sem):
    group = lax.axis_index("group")
    member = lax.axis_index("member")
    width = 4 * B

    def store(j):
        return pltpu.make_async_copy(
            total.at[:, j * width:(j + 1) * width], out.at[:, j * width:(j + 1) * width], out_sem.at[j]
        )

    load_blocks = pltpu.make_async_copy(blocks_in, blocks, blocks_sem)
    load_blocks.start()
    total[...] = front[...]
    load_blocks.wait()
    for j in range(2):
        run = 2 * group + j
        for g in range(8):
            for a in range(2):
                r = blocks[g, 2 * member + a] - SIDE * member
                for b in range(2):
                    c = blocks[g, 2 * run + b] - SIDE * run + SIDE * j
                    where = (pl.ds(pl.multiple_of(r * B, B), B), pl.ds(pl.multiple_of(c * B, B), B))
                    total[where] -= tiles[g, j, a * B:(a + 1) * B, b * B:(b + 1) * B].astype(jnp.float32)
        store(j).start()
    for j in range(2):
        store(j).wait()


def place(blocks, front, tiles):
    return pl.pallas_call(
        place_kernel,
        out_shape=jax.ShapeDtypeStruct(front.shape, jnp.float32),
        in_specs=[
            pl.BlockSpec(memory_space=pl.ANY),
            pl.BlockSpec(memory_space=pltpu.VMEM),
            pl.BlockSpec(memory_space=pltpu.VMEM),
        ],
        out_specs=pl.BlockSpec(memory_space=pl.ANY),
        scratch_shapes=[
            pltpu.SMEM(blocks.shape, jnp.int32),
            pltpu.VMEM(front.shape, jnp.float32),
            pltpu.SemaphoreType.DMA,
            pltpu.SemaphoreType.DMA((2,)),
        ],
        compiler_params=pltpu.CompilerParams(vmem_limit_bytes=32 * 2**20),
        name="place",
    )(blocks, front, tiles)


def local(root_front, child_panels, pivot_sizes, pivot_signs, child_blocks):
    kept = [pltpu.with_memory_space_constraint(x, pltpu.HBM) for x in (child_panels, pivot_sizes, pivot_signs)]
    tiles = meet(*kept)
    return place(child_blocks, root_front, tiles)


def solution(mesh):
    placed = (
        P("member", "group"),
        P("group", "member", None),
        P("group", None),
        P("group", None),
        P(),
    )
    return jax.shard_map(
        local, mesh=mesh, in_specs=placed, out_specs=P("member", "group"), check_vma=False
    )
```

```python
import jax
import jax.numpy as jnp
from jax import lax
from jax.experimental import pallas as pl
from jax.experimental.pallas import tpu as pltpu
from jax.sharding import PartitionSpec as P

B = 128
ROWS = 256
K = 4096
NC = 8
KC = K // NC
KH = 2 * KC
AHEAD = 3
SIDE = 4
pivot_floor = 0.1

CROSS = ((0, 0), (0, 1), (1, 0), (0, 3), (0, 2), (2, 0))
PAIRS = (
    (0, 0), (0, 1), (0, 2), (2, 1),
    (0, 3), (2, 3), (5, 3),
    (0, 4), (2, 4), (0, 5), (1, 5),
    (4, 5),
)
TILES = tuple((n, a, b, False) for n, (a, b) in enumerate(PAIRS) if n != 6) + tuple(
    (n, PAIRS[n][1], PAIRS[n][0], True) for n in (2, 3, 5, 6, 8)
)
SELF, NEAR, CORNER, FAR, LAST = (0,), (1, 2, 3), (4, 5, 6), (7, 8, 9, 10), (11,)
WHOLE = 2
QUARTERS = (3, 4)
LANE = (0, 1, 0, 1, 2)
PASS_NEAR, PASS_FAR = 2, 2
EARLY = 3


def dot_nt(left, right):
    return lax.dot_general(left, right, (((1,), (1,)), ((), ())), preferred_element_type=jnp.float32)


def half_rows(h):
    return pl.ds(h * B if isinstance(h, int) else pl.multiple_of(h * B, B), B)


def quarter(h):
    return pl.ds(B + (h - QUARTERS[0]) * (B // 2), B // 2)


def part(ref, flipped, h):
    if h == WHOLE:
        return ref
    if h in QUARTERS:
        return ref.at[quarter(h), :]
    return ref.at[half_rows(h), :] if flipped else ref.at[:, half_rows(h)]


def meet_kernel(
    panel, sizes_in, signs_in, arrived, pan, sizes, signs, acc, stage, mine,
    load_sem, row_sem, hop_send, hop_recv, relay_send, relay_recv, tile_send, tile_recv,
):
    group = lax.axis_index("group")
    member = lax.axis_index("member")
    row, col = member // SIDE, member % SIDE
    odd = group % 2

    def at(offset):
        across, along = offset
        y = (row + jnp.where(odd == 0, across, -along) + SIDE) % SIDE
        z = (col + jnp.where(odd == 0, along, -across) + SIDE) % SIDE
        return y * SIDE + z

    to_back, to_across, to_ahead = at((0, -1)), at((-1, 0)), at((0, 1))

    def cols(k):
        return pl.ds(pl.multiple_of(k * KC, KC), KC)

    def load(k):
        return pltpu.make_async_copy(panel.at[0, :, cols(k)], pan.at[0, :, cols(k)], load_sem.at[k])

    load_sizes = pltpu.make_async_copy(sizes_in, sizes, row_sem.at[0])
    load_signs = pltpu.make_async_copy(signs_in, signs, row_sem.at[1])
    load_sizes.start()
    for k in range(NC):
        load(k).start()
    load_signs.start()

    barrier = pltpu.get_barrier_semaphore()

    def greet(g, m):
        pl.semaphore_signal(
            barrier, inc=1, device_id={"group": g, "member": m}, device_id_type=pl.DeviceIdType.MESH
        )

    for offset in ((0, 1), (1, 0), (0, -1)):
        greet(group, at(offset))
    rows_of = sorted({r for _, r, _, _ in TILES if r != 0})
    for r in rows_of:
        greet(group, at((-CROSS[r][0], -CROSS[r][1])))
    for step in range(1, 8):
        greet((group + step) % 8, member)
    greeted = 3 + len(rows_of) + 7

    def hop(src, dst, rows, columns, n, target):
        return pltpu.make_async_remote_copy(
            src_ref=pan.at[src, rows, columns],
            dst_ref=pan.at[dst, rows, columns],
            send_sem=hop_send.at[dst - 1, n],
            recv_sem=hop_recv.at[dst - 1, n],
            device_id={"group": group, "member": target},
            device_id_type=pl.DeviceIdType.MESH,
        )

    def wide(kk):
        return pl.ds(pl.multiple_of(kk * KH, KH), KH)

    def hops_own(k):
        return hop(0, 1, slice(None), cols(k), k, to_back), hop(0, 2, slice(None), cols(k), k, to_across)

    def hops_far(f):
        rows, columns = half_rows(f // 4), wide(f % 4)
        return hop(1, 4, rows, columns, f, to_back), hop(2, 5, rows, columns, f, to_across)

    def hops_corner(c):
        if c < 2:
            return (
                hop(4, 3, half_rows(0), wide(c), c, to_back),
                hop(0, 3, half_rows(0), wide(2 + c), 2 + c, to_ahead),
            )
        rows = quarter(QUARTERS[c - 2])
        return (
            hop(4, 3, rows, pl.ds(0, K // 2), 2 * c, to_back),
            hop(0, 3, rows, pl.ds(K // 2, K // 2), 2 * c + 1, to_ahead),
        )

    def start(pair):
        for copy in pair:
            copy.start()

    def landed(pair):
        for copy in pair:
            copy.wait_recv()

    load_sizes.wait()
    root = jnp.sqrt(jnp.maximum(sizes[...], pivot_floor))
    for k in range(NC):
        load(k).wait()
        s = slice(k * KC, (k + 1) * KC)
        pan[0, :, s] = (pan[0, :, s].astype(jnp.float32) * root[:, s]).astype(jnp.bfloat16)
        if k == 0:
            pl.semaphore_wait(barrier, greeted)
        if k < AHEAD:
            start(hops_own(k))
    load_signs.wait()
    acc[...] = jnp.zeros_like(acc)

    def signed(slot, rows, columns):
        s = (2 * signs[:, columns] - 1).astype(jnp.float32).astype(jnp.bfloat16)
        return pan[slot, rows, columns] * s

    def accumulate(n, rows, columns, prod):
        acc[n, rows, columns] += prod

    def relay(slot, h):
        _, r, _, flipped = TILES[slot]
        return pltpu.make_async_remote_copy(
            src_ref=part(stage.at[slot], flipped, h),
            dst_ref=part(mine.at[slot], flipped, h),
            send_sem=relay_send.at[slot, LANE[h]],
            recv_sem=relay_recv.at[slot, LANE[h]],
            device_id={"group": group, "member": at(CROSS[r])},
            device_id_type=pl.DeviceIdType.MESH,
        )

    def home(slot):
        _, r, c, _ = TILES[slot]
        column = at((CROSS[c][0] - CROSS[r][0], CROSS[c][1] - CROSS[r][1]))
        return column // 2, column % 2

    def to_owner(slot, h):
        owner, side = home(slot)
        flipped = TILES[slot][3]
        return pltpu.make_async_remote_copy(
            src_ref=part(mine.at[slot], flipped, h),
            dst_ref=part(arrived.at[group, side], flipped, h),
            send_sem=tile_send.at[slot, LANE[h]],
            recv_sem=tile_recv.at[group, side],
            device_id={"group": owner, "member": member},
            device_id_type=pl.DeviceIdType.MESH,
        )

    def deliver(slot, h):
        owner, side = home(slot)
        flipped = TILES[slot][3]

        @pl.when(owner == group)
        def _():
            pltpu.make_async_copy(
                part(mine.at[slot], flipped, h),
                part(arrived.at[group, side], flipped, h),
                tile_recv.at[group, side],
            ).start()

        @pl.when(owner != group)
        def _():
            to_owner(slot, h).start()

    everything = slice(None)

    def parts_of(slot):
        n, _, _, flipped = TILES[slot]
        if n in SELF + NEAR + LAST:
            return (WHOLE,)
        return (0, *QUARTERS) if n in CORNER and flipped else (0, 1)

    def ship(products, h):
        for here in (False, True):
            for slot, (n, r, _, flipped) in enumerate(TILES):
                if n not in products or here != (r == 0) or h not in parts_of(slot):
                    continue
                columns = everything if h == WHOLE else quarter(h) if h in QUARTERS else half_rows(h)
                value = acc[n, :, columns].astype(jnp.bfloat16)
                part((mine if here else stage).at[slot], flipped, h)[...] = value.T if flipped else value
                if here:
                    deliver(slot, h)
                else:
                    relay(slot, h).start()

    def pass_on(products, h):
        for slot, (n, r, _, _) in enumerate(TILES):
            if n in products and r != 0 and h in parts_of(slot):
                relay(slot, h).wait_recv()
                deliver(slot, h)

    def near(k, carry):
        own = signed(0, everything, cols(k))
        landed(hops_own(k))

        @pl.when(k + AHEAD < NC)
        def _():
            start(hops_own(k + AHEAD))

        @pl.when(k + AHEAD >= NC)
        def _():
            start(hops_far(k + AHEAD - NC))

        accumulate(1, everything, everything, dot_nt(own, pan[1, :, cols(k)]))
        accumulate(2, everything, everything, dot_nt(own, pan[2, :, cols(k)]))
        accumulate(3, everything, everything, dot_nt(signed(2, everything, cols(k)), pan[1, :, cols(k)]))
        return carry

    def self_product(k, carry):
        accumulate(0, everything, everything, dot_nt(signed(0, everything, cols(k)), pan[0, :, cols(k)]))
        return carry

    lax.fori_loop(0, NC, self_product, 0)
    ship(SELF, WHOLE)
    lax.fori_loop(0, NC, near, 0)
    ship(NEAR, WHOLE)

    def far(h, kk):
        f = 4 * h + kk
        landed(hops_far(f))

        @pl.when(f + AHEAD < NC)
        def _():
            start(hops_far(f + AHEAD))

        for c in range(EARLY):

            @pl.when(f + AHEAD == NC + c)
            def _():
                start(hops_corner(c))

        here, where = half_rows(h), wide(kk)
        along = signed(4, here, where)
        accumulate(7, everything, here, dot_nt(pan[0, :, where], along))
        accumulate(8, everything, here, dot_nt(pan[2, :, where], along))
        across = signed(5, here, where)
        accumulate(9, everything, here, dot_nt(pan[0, :, where], across))
        accumulate(10, everything, here, dot_nt(pan[1, :, where], across))
        if h == 0:
            accumulate(11, here, here, dot_nt(pan[4, here, where], across))
        else:
            accumulate(11, everything, here, dot_nt(pan[4, :, where], across))
            accumulate(11, here, half_rows(0), dot_nt(along, pan[5, half_rows(0), where]))

    def far_first(kk, carry):
        far(0, kk)

        @pl.when(kk == PASS_NEAR)
        def _():
            pass_on(NEAR, WHOLE)

        return carry

    lax.fori_loop(0, 4, far_first, 0)
    ship(FAR, 0)

    def far_second(kk, carry):
        far(1, kk)

        @pl.when(kk == PASS_FAR)
        def _():
            pass_on(FAR, 0)

        return carry

    lax.fori_loop(0, 4, far_second, 0)
    ship(FAR, 1)
    ship(LAST, WHOLE)
    for c in range(EARLY, 4):
        start(hops_corner(c))

    def corner(c):
        landed(hops_corner(c))
        if c < 2:
            here, sides = half_rows(0), (wide(c), wide(2 + c))
        else:
            here, sides = quarter(QUARTERS[c - 2]), (pl.ds(0, K // 2), pl.ds(K // 2, K // 2))
        low, high = signed(3, here, sides[0]), signed(3, here, sides[1])
        for n in CORNER:
            left = PAIRS[n][0]
            prod = dot_nt(pan[left, :, sides[0]], low)
            prod += dot_nt(pan[left, :, sides[1]], high)
            accumulate(n, everything, here, prod)

    corner(0)
    corner(1)
    ship(CORNER, 0)
    pass_on(FAR, 1)
    pass_on(LAST, WHOLE)
    corner(2)
    ship(CORNER, 3)
    corner(3)
    pass_on(CORNER, 0)
    ship(CORNER, 4)
    ship(CORNER, 1)
    pass_on(CORNER, 3)
    pass_on(CORNER, 4)
    pass_on(CORNER, 1)

    def drain(k, carry):
        for copy in hops_own(k) + hops_far(k):
            copy.wait_send()
        return carry

    lax.fori_loop(0, NC, drain, 0)
    for c in range(4):
        for copy in hops_corner(c):
            copy.wait_send()
    for slot, (n, r, _, _) in enumerate(TILES):
        for h in parts_of(slot):
            if r != 0:
                relay(slot, h).wait_send()

            @pl.when(home(slot)[0] != group)
            def _():
                to_owner(slot, h).wait_send()

    for g in range(8):
        for j in range(2):
            pltpu.make_async_copy(mine.at[0], arrived.at[g, j], tile_recv.at[g, j]).wait()


def meet(panel, sizes, signs):
    return pl.pallas_call(
        meet_kernel,
        out_shape=jax.ShapeDtypeStruct((8, 2, ROWS, ROWS), jnp.bfloat16),
        in_specs=[pl.BlockSpec(memory_space=pltpu.HBM)] * 3,
        out_specs=pl.BlockSpec(memory_space=pl.ANY),
        scratch_shapes=[
            pltpu.VMEM((6, ROWS, K), jnp.bfloat16),
            pltpu.VMEM((1, K), jnp.float32),
            pltpu.VMEM((1, K), jnp.int32),
            pltpu.VMEM((12, ROWS, ROWS), jnp.float32),
            pltpu.VMEM((16, ROWS, ROWS), jnp.bfloat16),
            pltpu.VMEM((16, ROWS, ROWS), jnp.bfloat16),
            pltpu.SemaphoreType.DMA((NC,)),
            pltpu.SemaphoreType.DMA((2,)),
            pltpu.SemaphoreType.DMA((5, NC)),
            pltpu.SemaphoreType.DMA((5, NC)),
            pltpu.SemaphoreType.DMA((16, 3)),
            pltpu.SemaphoreType.DMA((16, 3)),
            pltpu.SemaphoreType.DMA((16, 3)),
            pltpu.SemaphoreType.DMA((8, 2)),
        ],
        compiler_params=pltpu.CompilerParams(
            collective_id=0, has_side_effects=True, vmem_limit_bytes=40 * 2**20
        ),
        name="meet",
    )(panel, sizes, signs)


def place_kernel(blocks_in, front, tiles, out, blocks, total, blocks_sem, out_sem):
    group = lax.axis_index("group")
    member = lax.axis_index("member")
    width = 4 * B

    def store(j):
        return pltpu.make_async_copy(
            total.at[:, j * width:(j + 1) * width], out.at[:, j * width:(j + 1) * width], out_sem.at[j]
        )

    load_blocks = pltpu.make_async_copy(blocks_in, blocks, blocks_sem)
    load_blocks.start()
    total[...] = front[...]
    load_blocks.wait()
    for j in range(2):
        run = 2 * group + j
        for g in range(8):
            for a in range(2):
                r = blocks[g, 2 * member + a] - SIDE * member
                for b in range(2):
                    c = blocks[g, 2 * run + b] - SIDE * run + SIDE * j
                    where = (pl.ds(pl.multiple_of(r * B, B), B), pl.ds(pl.multiple_of(c * B, B), B))
                    total[where] -= tiles[g, j, a * B:(a + 1) * B, b * B:(b + 1) * B].astype(jnp.float32)
        store(j).start()
    for j in range(2):
        store(j).wait()


def place(blocks, front, tiles):
    return pl.pallas_call(
        place_kernel,
        out_shape=jax.ShapeDtypeStruct(front.shape, jnp.float32),
        in_specs=[
            pl.BlockSpec(memory_space=pl.ANY),
            pl.BlockSpec(memory_space=pltpu.VMEM),
            pl.BlockSpec(memory_space=pltpu.VMEM),
        ],
        out_specs=pl.BlockSpec(memory_space=pl.ANY),
        scratch_shapes=[
            pltpu.SMEM(blocks.shape, jnp.int32),
            pltpu.VMEM(front.shape, jnp.float32),
            pltpu.SemaphoreType.DMA,
            pltpu.SemaphoreType.DMA((2,)),
        ],
        compiler_params=pltpu.CompilerParams(vmem_limit_bytes=32 * 2**20),
        name="place",
    )(blocks, front, tiles)


def local(root_front, child_panels, pivot_sizes, pivot_signs, child_blocks):
    kept = [pltpu.with_memory_space_constraint(x, pltpu.HBM) for x in (child_panels, pivot_sizes, pivot_signs)]
    tiles = meet(*kept)
    return place(child_blocks, root_front, tiles)


def solution(mesh):
    placed = (
        P("member", "group"),
        P("group", "member", None),
        P("group", None),
        P("group", None),
        P(),
    )
    return jax.shard_map(
        local, mesh=mesh, in_specs=placed, out_specs=P("member", "group"), check_vma=False
    )
```

```python
import jax
import jax.numpy as jnp
from jax import lax
from jax.experimental import pallas as pl
from jax.experimental.pallas import tpu as pltpu
from jax.sharding import PartitionSpec as P

B = 128
ROWS = 256
K = 4096
NC = 8
KC = K // NC
KH = 2 * KC
AHEAD = 3
SIDE = 4
pivot_floor = 0.1

CROSS = ((0, 0), (0, 1), (1, 0), (0, 3), (0, 2), (2, 0))
PAIRS = (
    (0, 0), (0, 1), (0, 2), (2, 1),
    (0, 3), (2, 3), (5, 3),
    (0, 4), (2, 4), (0, 5), (1, 5),
    (4, 5),
)
TILES = tuple((n, a, b, False) for n, (a, b) in enumerate(PAIRS) if n != 6) + tuple(
    (n, PAIRS[n][1], PAIRS[n][0], True) for n in (2, 3, 5, 6, 8)
)
SELF, NEAR, CORNER, FAR, LAST = (0,), (1, 2, 3), (4, 5, 6), (7, 8, 9, 10), (11,)
WHOLE = 2
PASS_NEAR, PASS_FAR = 2, 2
EARLY = 3


def dot_nt(left, right):
    return lax.dot_general(left, right, (((1,), (1,)), ((), ())), preferred_element_type=jnp.float32)


def half_rows(h):
    return pl.ds(h * B if isinstance(h, int) else pl.multiple_of(h * B, B), B)


def part(ref, flipped, h):
    if h == WHOLE:
        return ref
    return ref.at[half_rows(h), :] if flipped else ref.at[:, half_rows(h)]


def meet_kernel(
    panel, sizes_in, signs_in, arrived, pan, sizes, signs, acc, stage, mine,
    load_sem, row_sem, hop_send, hop_recv, relay_send, relay_recv, tile_send, tile_recv,
):
    group = lax.axis_index("group")
    member = lax.axis_index("member")
    row, col = member // SIDE, member % SIDE
    odd = group % 2

    def at(offset):
        across, along = offset
        y = (row + jnp.where(odd == 0, across, -along) + SIDE) % SIDE
        z = (col + jnp.where(odd == 0, along, -across) + SIDE) % SIDE
        return y * SIDE + z

    to_back, to_across, to_ahead = at((0, -1)), at((-1, 0)), at((0, 1))

    def cols(k):
        return pl.ds(pl.multiple_of(k * KC, KC), KC)

    def load(k):
        return pltpu.make_async_copy(panel.at[0, :, cols(k)], pan.at[0, :, cols(k)], load_sem.at[k])

    load_sizes = pltpu.make_async_copy(sizes_in, sizes, row_sem.at[0])
    load_signs = pltpu.make_async_copy(signs_in, signs, row_sem.at[1])
    load_sizes.start()
    for k in range(NC):
        load(k).start()
    load_signs.start()

    barrier = pltpu.get_barrier_semaphore()

    def greet(g, m):
        pl.semaphore_signal(
            barrier, inc=1, device_id={"group": g, "member": m}, device_id_type=pl.DeviceIdType.MESH
        )

    for offset in ((0, 1), (1, 0), (0, -1)):
        greet(group, at(offset))
    rows_of = sorted({r for _, r, _, _ in TILES if r != 0})
    for r in rows_of:
        greet(group, at((-CROSS[r][0], -CROSS[r][1])))
    for step in range(1, 8):
        greet((group + step) % 8, member)
    greeted = 3 + len(rows_of) + 7

    def hop(src, dst, rows, columns, n, target):
        return pltpu.make_async_remote_copy(
            src_ref=pan.at[src, rows, columns],
            dst_ref=pan.at[dst, rows, columns],
            send_sem=hop_send.at[dst - 1, n],
            recv_sem=hop_recv.at[dst - 1, n],
            device_id={"group": group, "member": target},
            device_id_type=pl.DeviceIdType.MESH,
        )

    def wide(kk):
        return pl.ds(pl.multiple_of(kk * KH, KH), KH)

    def hops_own(k):
        return hop(0, 1, slice(None), cols(k), k, to_back), hop(0, 2, slice(None), cols(k), k, to_across)

    def hops_far(f):
        rows, columns = half_rows(f // 4), wide(f % 4)
        return hop(1, 4, rows, columns, f, to_back), hop(2, 5, rows, columns, f, to_across)

    def hops_corner(c):
        h, i = c // 2, c % 2
        return (
            hop(4, 3, half_rows(h), wide(i), 4 * h + i, to_back),
            hop(0, 3, half_rows(h), wide(2 + i), 4 * h + 2 + i, to_ahead),
        )

    def start(pair):
        for copy in pair:
            copy.start()

    def landed(pair):
        for copy in pair:
            copy.wait_recv()

    load_sizes.wait()
    root = jnp.sqrt(jnp.maximum(sizes[...], pivot_floor))
    for k in range(NC):
        load(k).wait()
        s = slice(k * KC, (k + 1) * KC)
        pan[0, :, s] = (pan[0, :, s].astype(jnp.float32) * root[:, s]).astype(jnp.bfloat16)
        if k == 0:
            pl.semaphore_wait(barrier, greeted)
        if k < AHEAD:
            start(hops_own(k))
    load_signs.wait()
    acc[...] = jnp.zeros_like(acc)

    def signed(slot, rows, columns):
        s = (2 * signs[:, columns] - 1).astype(jnp.float32).astype(jnp.bfloat16)
        return pan[slot, rows, columns] * s

    def accumulate(n, rows, columns, prod):
        acc[n, rows, columns] += prod

    def relay(slot, h):
        _, r, _, flipped = TILES[slot]
        return pltpu.make_async_remote_copy(
            src_ref=part(stage.at[slot], flipped, h),
            dst_ref=part(mine.at[slot], flipped, h),
            send_sem=relay_send.at[slot, h % 2],
            recv_sem=relay_recv.at[slot, h % 2],
            device_id={"group": group, "member": at(CROSS[r])},
            device_id_type=pl.DeviceIdType.MESH,
        )

    def home(slot):
        _, r, c, _ = TILES[slot]
        column = at((CROSS[c][0] - CROSS[r][0], CROSS[c][1] - CROSS[r][1]))
        return column // 2, column % 2

    def to_owner(slot, h):
        owner, side = home(slot)
        flipped = TILES[slot][3]
        return pltpu.make_async_remote_copy(
            src_ref=part(mine.at[slot], flipped, h),
            dst_ref=part(arrived.at[group, side], flipped, h),
            send_sem=tile_send.at[slot, h % 2],
            recv_sem=tile_recv.at[group, side],
            device_id={"group": owner, "member": member},
            device_id_type=pl.DeviceIdType.MESH,
        )

    def deliver(slot, h):
        owner, side = home(slot)
        flipped = TILES[slot][3]

        @pl.when(owner == group)
        def _():
            pltpu.make_async_copy(
                part(mine.at[slot], flipped, h),
                part(arrived.at[group, side], flipped, h),
                tile_recv.at[group, side],
            ).start()

        @pl.when(owner != group)
        def _():
            to_owner(slot, h).start()

    def ship(products, h):
        for here in (False, True):
            for slot, (n, r, _, flipped) in enumerate(TILES):
                if n not in products or here != (r == 0):
                    continue
                value = (acc[n] if h == WHOLE else acc[n, :, half_rows(h)]).astype(jnp.bfloat16)
                part((mine if here else stage).at[slot], flipped, h)[...] = value.T if flipped else value
                if here:
                    deliver(slot, h)
                else:
                    relay(slot, h).start()

    def pass_on(products, h):
        for slot, (n, r, _, _) in enumerate(TILES):
            if n in products and r != 0:
                relay(slot, h).wait_recv()
                deliver(slot, h)

    everything = slice(None)

    def near(k, carry):
        own = signed(0, everything, cols(k))
        landed(hops_own(k))

        @pl.when(k + AHEAD < NC)
        def _():
            start(hops_own(k + AHEAD))

        @pl.when(k + AHEAD >= NC)
        def _():
            start(hops_far(k + AHEAD - NC))

        accumulate(1, everything, everything, dot_nt(own, pan[1, :, cols(k)]))
        accumulate(2, everything, everything, dot_nt(own, pan[2, :, cols(k)]))
        accumulate(3, everything, everything, dot_nt(signed(2, everything, cols(k)), pan[1, :, cols(k)]))
        return carry

    def self_product(k, carry):
        accumulate(0, everything, everything, dot_nt(signed(0, everything, cols(k)), pan[0, :, cols(k)]))
        return carry

    lax.fori_loop(0, NC, self_product, 0)
    ship(SELF, WHOLE)
    lax.fori_loop(0, NC, near, 0)
    ship(NEAR, WHOLE)

    def far(h, kk):
        f = 4 * h + kk
        landed(hops_far(f))

        @pl.when(f + AHEAD < NC)
        def _():
            start(hops_far(f + AHEAD))

        @pl.when(jnp.logical_and(f + AHEAD >= NC, f + AHEAD < NC + EARLY))
        def _():
            start(hops_corner(f + AHEAD - NC))

        here, where = half_rows(h), wide(kk)
        along = signed(4, here, where)
        accumulate(7, everything, here, dot_nt(pan[0, :, where], along))
        accumulate(8, everything, here, dot_nt(pan[2, :, where], along))
        across = signed(5, here, where)
        accumulate(9, everything, here, dot_nt(pan[0, :, where], across))
        accumulate(10, everything, here, dot_nt(pan[1, :, where], across))
        if h == 0:
            accumulate(11, here, here, dot_nt(pan[4, here, where], across))
        else:
            accumulate(11, everything, here, dot_nt(pan[4, :, where], across))
            accumulate(11, here, half_rows(0), dot_nt(along, pan[5, half_rows(0), where]))

    def far_first(kk, carry):
        far(0, kk)

        @pl.when(kk == PASS_NEAR)
        def _():
            pass_on(NEAR, WHOLE)

        return carry

    lax.fori_loop(0, 4, far_first, 0)
    ship(FAR, 0)

    def far_second(kk, carry):
        far(1, kk)

        @pl.when(kk == PASS_FAR)
        def _():
            pass_on(FAR, 0)

        return carry

    lax.fori_loop(0, 4, far_second, 0)
    ship(FAR, 1)
    ship(LAST, WHOLE)
    for c in range(EARLY, 4):
        start(hops_corner(c))

    def corner(h, i):
        landed(hops_corner(2 * h + i))
        here = half_rows(h)
        low, high = signed(3, here, wide(i)), signed(3, here, wide(2 + i))
        for n in CORNER:
            left = PAIRS[n][0]
            prod = dot_nt(pan[left, :, wide(i)], low)
            prod += dot_nt(pan[left, :, wide(2 + i)], high)
            accumulate(n, everything, here, prod)

    corner(0, 0)
    corner(0, 1)
    ship(CORNER, 0)
    corner(1, 0)
    pass_on(FAR, 1)
    pass_on(LAST, WHOLE)
    corner(1, 1)
    pass_on(CORNER, 0)
    ship(CORNER, 1)
    pass_on(CORNER, 1)

    def drain(k, carry):
        for copy in hops_own(k) + hops_far(k):
            copy.wait_send()
        return carry

    lax.fori_loop(0, NC, drain, 0)
    for c in range(4):
        for copy in hops_corner(c):
            copy.wait_send()
    for slot, (n, r, _, _) in enumerate(TILES):
        for h in (WHOLE,) if n in SELF + NEAR + LAST else (0, 1):
            if r != 0:
                relay(slot, h).wait_send()

            @pl.when(home(slot)[0] != group)
            def _():
                to_owner(slot, h).wait_send()

    for g in range(8):
        for j in range(2):
            pltpu.make_async_copy(mine.at[0], arrived.at[g, j], tile_recv.at[g, j]).wait()


def meet(panel, sizes, signs):
    return pl.pallas_call(
        meet_kernel,
        out_shape=jax.ShapeDtypeStruct((8, 2, ROWS, ROWS), jnp.bfloat16),
        in_specs=[pl.BlockSpec(memory_space=pltpu.HBM)] * 3,
        out_specs=pl.BlockSpec(memory_space=pl.ANY),
        scratch_shapes=[
            pltpu.VMEM((6, ROWS, K), jnp.bfloat16),
            pltpu.VMEM((1, K), jnp.float32),
            pltpu.VMEM((1, K), jnp.int32),
            pltpu.VMEM((12, ROWS, ROWS), jnp.float32),
            pltpu.VMEM((16, ROWS, ROWS), jnp.bfloat16),
            pltpu.VMEM((16, ROWS, ROWS), jnp.bfloat16),
            pltpu.SemaphoreType.DMA((NC,)),
            pltpu.SemaphoreType.DMA((2,)),
            pltpu.SemaphoreType.DMA((5, NC)),
            pltpu.SemaphoreType.DMA((5, NC)),
            pltpu.SemaphoreType.DMA((16, 2)),
            pltpu.SemaphoreType.DMA((16, 2)),
            pltpu.SemaphoreType.DMA((16, 2)),
            pltpu.SemaphoreType.DMA((8, 2)),
        ],
        compiler_params=pltpu.CompilerParams(
            collective_id=0, has_side_effects=True, vmem_limit_bytes=40 * 2**20
        ),
        name="meet",
    )(panel, sizes, signs)


def place_kernel(blocks_in, front, tiles, out, blocks, total, blocks_sem, out_sem):
    group = lax.axis_index("group")
    member = lax.axis_index("member")
    width = 4 * B

    def store(j):
        return pltpu.make_async_copy(
            total.at[:, j * width:(j + 1) * width], out.at[:, j * width:(j + 1) * width], out_sem.at[j]
        )

    load_blocks = pltpu.make_async_copy(blocks_in, blocks, blocks_sem)
    load_blocks.start()
    total[...] = front[...]
    load_blocks.wait()
    for j in range(2):
        run = 2 * group + j
        for g in range(8):
            for a in range(2):
                r = blocks[g, 2 * member + a] - SIDE * member
                for b in range(2):
                    c = blocks[g, 2 * run + b] - SIDE * run + SIDE * j
                    where = (pl.ds(pl.multiple_of(r * B, B), B), pl.ds(pl.multiple_of(c * B, B), B))
                    total[where] -= tiles[g, j, a * B:(a + 1) * B, b * B:(b + 1) * B].astype(jnp.float32)
        store(j).start()
    for j in range(2):
        store(j).wait()


def place(blocks, front, tiles):
    return pl.pallas_call(
        place_kernel,
        out_shape=jax.ShapeDtypeStruct(front.shape, jnp.float32),
        in_specs=[
            pl.BlockSpec(memory_space=pl.ANY),
            pl.BlockSpec(memory_space=pltpu.VMEM),
            pl.BlockSpec(memory_space=pltpu.VMEM),
        ],
        out_specs=pl.BlockSpec(memory_space=pl.ANY),
        scratch_shapes=[
            pltpu.SMEM(blocks.shape, jnp.int32),
            pltpu.VMEM(front.shape, jnp.float32),
            pltpu.SemaphoreType.DMA,
            pltpu.SemaphoreType.DMA((2,)),
        ],
        compiler_params=pltpu.CompilerParams(vmem_limit_bytes=32 * 2**20),
        name="place",
    )(blocks, front, tiles)


def local(root_front, child_panels, pivot_sizes, pivot_signs, child_blocks):
    kept = [pltpu.with_memory_space_constraint(x, pltpu.HBM) for x in (child_panels, pivot_sizes, pivot_signs)]
    tiles = meet(*kept)
    return place(child_blocks, root_front, tiles)


def solution(mesh):
    placed = (
        P("member", "group"),
        P("group", "member", None),
        P("group", None),
        P("group", None),
        P(),
    )
    return jax.shard_map(
        local, mesh=mesh, in_specs=placed, out_specs=P("member", "group"), check_vma=False
    )
```
